32 devices in a mesh: cohort: 4 (over x, core), person: 8 (over z, y).
Axes of the slice: x: 2, y: 2, z: 4, core: 2. Of those that a mesh axis runs over, the one named last changes fastest.
Arguments:
- dosages: bfloat16 [4, 1024, 1536], P('cohort', 'person'), may hold values from 0 to 2
- allele_counts: int32 [4, 8, 1536], P('cohort', 'person'), may hold values from 0 to 256, as said below
- partner: int32 [4], replicated, may hold values from 0 to 3, as said below
Outputs:
- relation: bfloat16 [4, 1024, 1024], P('cohort', 'person')
The draws below stay inside these ranges and needn't reach their ends.
Inputs may be any that keep to these rules, and one draw needn't show every extreme that they name: `allele_counts`: each entry lies between 0 and 256, and some entry equals 256. partner[c] = c XOR r for one round number r with 1 <= r < 4, the same for every c.
All inputs are finite; a program needn't handle non-finite values.
Results may differ from the reference program's by a relative error of at most 0.0058.
Values may be sent and summed in bfloat16 or wider, within the bound.
No kernel may reach another device: no remote copies, remote signals or barrier semaphores. Data moves between devices by JAX's collectives and lax.ppermute only.
A program may use at most 64 MiB of HBM per device.

```python
import math
import jax
import jax.numpy as jnp
from jax import lax

PEOPLE_DEV = 128
MARKERS = 1536
BLOCKS = 8
PEOPLE = 1024
COHORTS = 4


def block_counts(key):
    first, second, third = jax.random.split(key, 3)
    quarter = PEOPLE_DEV // 4
    base = jax.random.randint(first, (COHORTS, 1, MARKERS), quarter, 2 * PEOPLE_DEV - quarter + 1)
    jitter = jax.random.randint(second, (COHORTS, BLOCKS, MARKERS), -(PEOPLE_DEV // 8), PEOPLE_DEV // 8 + 1)
    counts = jnp.clip(base + jitter, 0, 2 * PEOPLE_DEV)
    place = jax.random.randint(third, (), 0, MARKERS)
    return counts.at[0, 0, place].set(2 * PEOPLE_DEV).astype(jnp.int32)


def draw_allele_counts(key, part):
    return block_counts(key)


def draw_dosages(key, part):
    counts = block_counts(key)
    key = jax.random.fold_in(key, 5)
    centre = counts.astype(jnp.float32) / PEOPLE_DEV
    centre = jnp.repeat(centre, PEOPLE_DEV, axis=1)
    noise = 0.5 * jax.random.normal(key, (COHORTS, PEOPLE, MARKERS), jnp.float32)
    return jnp.clip(centre + noise, 0.0, 2.0).astype(jnp.bfloat16)


def draw_partner(key, part):
    key = jax.random.fold_in(key, 23)
    round_number = jax.random.randint(key, (), 1, COHORTS)
    return jnp.bitwise_xor(jnp.arange(COHORTS, dtype=jnp.int32), round_number).astype(jnp.int32)


def setup_inputs(seed: int = 0) -> dict:
    splits = jax.random.split(jax.random.key(seed), 4)
    dosages = draw_dosages(jax.random.fold_in(splits[3], 71), 0)
    allele_counts = draw_allele_counts(jax.random.fold_in(splits[3], 71), 0)
    partner = draw_partner(jax.random.fold_in(splits[3], 71), 0)
    return dict(dosages=dosages, allele_counts=allele_counts, partner=partner)


def standardize(dosage_rows, count_rows):
    totals = lax.optimization_barrier(jnp.sum(count_rows, axis=0)).astype(jnp.int32)
    freq = (totals.astype(jnp.float32) + 1.0) / (2.0 * PEOPLE + 2.0)
    spread = jnp.sqrt(2.0 * freq * (1.0 - freq))
    return ((dosage_rows.astype(jnp.float32) - 2.0 * freq) / spread).astype(jnp.bfloat16)

def reference(dosages, allele_counts, partner):
    standard = jax.vmap(standardize)(dosages, allele_counts)
    root = math.sqrt(MARKERS)

    def one_cohort(cohort_index):
        mine = standard[cohort_index].astype(jnp.float32)
        theirs = standard[partner[cohort_index]].astype(jnp.float32)
        product = lax.dot_general(mine, theirs, (((1,), (1,)), ((), ())), preferred_element_type=jnp.float32)
        return (product / root).astype(jnp.bfloat16)
    return lax.map(one_cohort, jnp.arange(COHORTS, dtype=jnp.int32))
```

```python
import functools
import math

import jax
import jax.numpy as jnp
from jax import lax
from jax.experimental import pallas as pl
from jax.experimental.pallas import tpu as pltpu
from jax.sharding import PartitionSpec as P

AXES = ("cohort", "person")
VMEM_BYTES = 48 * 1024 * 1024


def left_cohorts(cohorts, round_number):
    if round_number == 1:
        return [c for c in range(cohorts) if c & 1 == 0]
    top = 1 << (round_number.bit_length() - 1)
    return [
        c
        for c in range(cohorts)
        if (c & top == 0 and c & 1 == 0) or (c & top and (c ^ round_number ^ 1) & 1 == 0)
    ]


def group_size(blocks):
    return 1 << (blocks.bit_length() // 2)


def standard_rows(rows, totals, people_all):
    freq = (totals.astype(jnp.float32) + 1.0) / (2.0 * people_all + 2.0)
    scale = 1.0 / jnp.sqrt(2.0 * freq * (1.0 - freq))
    return ((rows.astype(jnp.float32) - 2.0 * freq) * scale).astype(jnp.bfloat16)


def tile_kernel(near, far, people_all, root, *refs):
    lefts, rights = refs[:near], refs[near : near + far]
    left_totals, right_totals, left_out, right_out, left_std, right_std = refs[near + far :]
    rows = lefts[0].shape[0]
    for m in range(far):
        right_std[m * rows : (m + 1) * rows, :] = standard_rows(
            rights[m][...], right_totals[...], people_all
        )
    for d in range(near):
        left_std[d * rows : (d + 1) * rows, :] = standard_rows(
            lefts[d][...], left_totals[...], people_all
        )
    contract = (((1,), (1,)), ((), ()))
    for d in range(near):
        product = lax.dot_general(
            left_std[d * rows : (d + 1) * rows, :],
            right_std[...],
            contract,
            preferred_element_type=jnp.float32,
        )
        left_out[d] = (product / root).astype(jnp.bfloat16)
    for m in range(far):
        product = lax.dot_general(
            right_std[m * rows : (m + 1) * rows, :],
            left_std[...],
            contract,
            preferred_element_type=jnp.float32,
        )
        right_out[m] = (product / root).astype(jnp.bfloat16)


def tile(lefts, rights, left_totals, right_totals, people_all):
    near, far = len(lefts), len(rights)
    rows, markers = lefts[0].shape
    return pl.pallas_call(
        functools.partial(tile_kernel, near, far, people_all, math.sqrt(markers)),
        out_shape=(
            jax.ShapeDtypeStruct((near, rows, far * rows), jnp.bfloat16),
            jax.ShapeDtypeStruct((far, rows, near * rows), jnp.bfloat16),
        ),
        scratch_shapes=[
            pltpu.VMEM((near * rows, markers), jnp.bfloat16),
            pltpu.VMEM((far * rows, markers), jnp.bfloat16),
        ],
        compiler_params=pltpu.CompilerParams(vmem_limit_bytes=VMEM_BYTES),
    )(*lefts, *rights, left_totals, right_totals)


def place_kernel(near, far, where_ref, *refs):
    left_parts, right_parts, out_ref = refs[:near], refs[near : near + far], refs[near + far]
    rows = out_ref.shape[1]
    place = where_ref[1]

    def columns(d, m):
        block = jnp.bitwise_xor(place, d + near * m)
        return pl.ds(pl.multiple_of(block * rows, rows), rows)

    @pl.when(where_ref[0] == 1)
    def _():
        for d in range(near):
            for m in range(far):
                out_ref[0, :, columns(d, m)] = left_parts[d][:, m * rows : (m + 1) * rows]

    @pl.when(where_ref[0] == 0)
    def _():
        for d in range(near):
            for m in range(far):
                out_ref[0, :, columns(d, m)] = right_parts[m][:, d * rows : (d + 1) * rows]


def place_blocks(is_left, place, left_parts, right_parts):
    near, far = len(left_parts), len(right_parts)
    rows = left_parts[0].shape[0]
    where = jnp.stack([is_left.astype(jnp.int32), place])
    vmem = pl.BlockSpec(memory_space=pltpu.VMEM)
    return pl.pallas_call(
        functools.partial(place_kernel, near, far),
        out_shape=jax.ShapeDtypeStruct((1, rows, near * far * rows), jnp.bfloat16),
        in_specs=[pl.BlockSpec(memory_space=pltpu.SMEM)] + [vmem] * (near + far),
        out_specs=vmem,
        compiler_params=pltpu.CompilerParams(vmem_limit_bytes=VMEM_BYTES),
    )(where, *left_parts, *right_parts)


def one_round(round_number, cohorts, blocks, dosages, allele_counts):
    own = dosages[0]
    people_all = own.shape[0] * blocks
    near = group_size(blocks)
    far = blocks // near
    left = left_cohorts(cohorts, round_number)

    def among_left(d):
        return [(c * blocks + i, c * blocks + (i ^ d)) for c in left for i in range(blocks)]

    def to_left(m):
        return [
            ((c ^ round_number) * blocks + (i ^ near * m), c * blocks + i)
            for c in left
            for i in range(blocks)
        ]

    def from_left(m):
        return [(b, a) for a, b in to_left(m)]

    lefts = [own] + [lax.ppermute(own, AXES, among_left(d)) for d in range(1, near)]
    rights = [lax.ppermute(own, AXES, to_left(m)) for m in range(far)]
    totals = lax.psum(allele_counts[0], "person")
    right_totals = lax.ppermute(totals, AXES, to_left(0))
    left_out, right_out = tile(lefts, rights, totals, right_totals, people_all)
    left_parts = [left_out[0]] + [
        lax.ppermute(left_out[d], AXES, among_left(d)) for d in range(1, near)
    ]
    right_parts = [lax.ppermute(right_out[m], AXES, from_left(m)) for m in range(far)]
    cohort = lax.axis_index("cohort")
    is_left = functools.reduce(jnp.logical_or, [cohort == c for c in left])
    return place_blocks(is_left, lax.axis_index("person"), left_parts, right_parts)


def on_device(dosages, allele_counts, partner):
    cohorts, blocks = lax.axis_size("cohort"), lax.axis_size("person")
    rounds = [
        functools.partial(one_round, round_number, cohorts, blocks)
        for round_number in range(1, cohorts)
    ]
    return lax.switch(partner[0] - 1, rounds, dosages, allele_counts)


def solution(mesh):
    placed = (P("cohort", "person", None), P("cohort", "person", None), P())
    return jax.shard_map(
        on_device,
        mesh=mesh,
        in_specs=placed,
        out_specs=P("cohort", "person", None),
        check_vma=False,
    )
```

```python
import functools
import math

import jax
import jax.numpy as jnp
from jax import lax
from jax.experimental import pallas as pl
from jax.experimental.pallas import tpu as pltpu
from jax.sharding import PartitionSpec as P

AXES = ("cohort", "person")
VMEM_BYTES = 48 * 1024 * 1024


def left_cohorts(cohorts, round_number):
    if round_number == 1:
        return [c for c in range(cohorts) if c & 1 == 0]
    top = 1 << (round_number.bit_length() - 1)
    return [
        c
        for c in range(cohorts)
        if (c & top == 0 and c & 1 == 0) or (c & top and (c ^ round_number ^ 1) & 1 == 0)
    ]


def group_size(blocks):
    return 1 << (blocks.bit_length() // 2)


def standard_rows(rows, totals, people_all):
    freq = (totals.astype(jnp.float32) + 1.0) / (2.0 * people_all + 2.0)
    scale = 1.0 / jnp.sqrt(2.0 * freq * (1.0 - freq))
    return ((rows.astype(jnp.float32) - 2.0 * freq) * scale).astype(jnp.bfloat16)


def tile_kernel(near, far, people_all, root, *refs):
    lefts, rights = refs[:near], refs[near : near + far]
    left_totals, right_totals, left_out, right_out, left_std, right_std = refs[near + far :]
    rows = lefts[0].shape[0]
    for m in range(far):
        right_std[m * rows : (m + 1) * rows, :] = standard_rows(
            rights[m][...], right_totals[...], people_all
        )
    for d in range(near):
        left_std[d * rows : (d + 1) * rows, :] = standard_rows(
            lefts[d][...], left_totals[...], people_all
        )
    contract = (((1,), (1,)), ((), ()))
    for d in range(near):
        product = lax.dot_general(
            left_std[d * rows : (d + 1) * rows, :],
            right_std[...],
            contract,
            preferred_element_type=jnp.float32,
        )
        left_out[d] = (product / root).astype(jnp.bfloat16)
    for m in range(far):
        product = lax.dot_general(
            right_std[m * rows : (m + 1) * rows, :],
            left_std[...],
            contract,
            preferred_element_type=jnp.float32,
        )
        right_out[m] = (product / root).astype(jnp.bfloat16)


def tile(lefts, rights, left_totals, right_totals, people_all):
    near, far = len(lefts), len(rights)
    rows, markers = lefts[0].shape
    return pl.pallas_call(
        functools.partial(tile_kernel, near, far, people_all, math.sqrt(markers)),
        out_shape=(
            jax.ShapeDtypeStruct((near, rows, far * rows), jnp.bfloat16),
            jax.ShapeDtypeStruct((far, rows, near * rows), jnp.bfloat16),
        ),
        scratch_shapes=[
            pltpu.VMEM((near * rows, markers), jnp.bfloat16),
            pltpu.VMEM((far * rows, markers), jnp.bfloat16),
        ],
        compiler_params=pltpu.CompilerParams(vmem_limit_bytes=VMEM_BYTES),
    )(*lefts, *rights, left_totals, right_totals)


def place_kernel(near, far, where_ref, *refs):
    left_parts, right_parts, out_ref = refs[:near], refs[near : near + far], refs[near + far]
    rows = out_ref.shape[1]
    place = where_ref[1]

    def columns(d, m):
        block = jnp.bitwise_xor(place, d + near * m)
        return pl.ds(pl.multiple_of(block * rows, rows), rows)

    @pl.when(where_ref[0] == 1)
    def _():
        for d in range(near):
            for m in range(far):
                out_ref[0, :, columns(d, m)] = left_parts[d][:, m * rows : (m + 1) * rows]

    @pl.when(where_ref[0] == 0)
    def _():
        for d in range(near):
            for m in range(far):
                out_ref[0, :, columns(d, m)] = right_parts[m][:, d * rows : (d + 1) * rows]


def place_blocks(is_left, place, left_parts, right_parts):
    near, far = len(left_parts), len(right_parts)
    rows = left_parts[0].shape[0]
    where = jnp.stack([is_left.astype(jnp.int32), place])
    vmem = pl.BlockSpec(memory_space=pltpu.VMEM)
    return pl.pallas_call(
        functools.partial(place_kernel, near, far),
        out_shape=jax.ShapeDtypeStruct((1, rows, near * far * rows), jnp.bfloat16),
        in_specs=[pl.BlockSpec(memory_space=pltpu.SMEM)] + [vmem] * (near + far),
        out_specs=vmem,
        compiler_params=pltpu.CompilerParams(vmem_limit_bytes=VMEM_BYTES),
    )(where, *left_parts, *right_parts)


def one_round(round_number, cohorts, blocks, dosages, allele_counts):
    own = dosages[0]
    people_all = own.shape[0] * blocks
    near = group_size(blocks)
    far = blocks // near
    left = left_cohorts(cohorts, round_number)

    def among_left(d):
        return [
            (c * blocks + i, c * blocks + (i ^ d if c in left else i))
            for c in range(cohorts)
            for i in range(blocks)
        ]

    def to_left(m):
        pairs = []
        for c in left:
            for i in range(blocks):
                pairs.append(((c ^ round_number) * blocks + (i ^ near * m), c * blocks + i))
                pairs.append((c * blocks + i, (c ^ 1) * blocks + i))
        return pairs

    def from_left(m):
        return [(b, a) for a, b in to_left(m)]

    swap = [(c, c ^ round_number) for c in range(cohorts)]
    partner_counts = lax.ppermute(allele_counts[0], "cohort", swap)
    lefts = [own] + [lax.ppermute(own, AXES, among_left(d)) for d in range(1, near)]
    rights = [lax.ppermute(own, AXES, to_left(m)) for m in range(far)]
    totals = lax.psum(jnp.concatenate([allele_counts[0], partner_counts]), "person")
    left_out, right_out = tile(lefts, rights, totals[:1], totals[1:], people_all)
    left_parts = [left_out[0]] + [
        lax.ppermute(left_out[d], AXES, among_left(d)) for d in range(1, near)
    ]
    right_parts = [lax.ppermute(right_out[m], AXES, from_left(m)) for m in range(far)]
    cohort = lax.axis_index("cohort")
    is_left = functools.reduce(jnp.logical_or, [cohort == c for c in left])
    return place_blocks(is_left, lax.axis_index("person"), left_parts, right_parts)


def on_device(dosages, allele_counts, partner):
    cohorts, blocks = lax.axis_size("cohort"), lax.axis_size("person")
    rounds = [
        functools.partial(one_round, round_number, cohorts, blocks)
        for round_number in range(1, cohorts)
    ]
    return lax.switch(partner[0] - 1, rounds, dosages, allele_counts)


def solution(mesh):
    placed = (P("cohort", "person", None), P("cohort", "person", None), P())
    return jax.shard_map(
        on_device,
        mesh=mesh,
        in_specs=placed,
        out_specs=P("cohort", "person", None),
        check_vma=False,
    )
```

```python
import functools
import math

import jax
import jax.numpy as jnp
from jax import lax
from jax.experimental import pallas as pl
from jax.experimental.pallas import tpu as pltpu
from jax.sharding import PartitionSpec as P

AXES = ("cohort", "person")
VMEM_BYTES = 48 * 1024 * 1024


def left_cohorts(cohorts, round_number):
    if round_number == 1:
        return [c for c in range(cohorts) if c & 1 == 0]
    top = 1 << (round_number.bit_length() - 1)
    return [
        c
        for c in range(cohorts)
        if (c & top == 0 and c & 1 == 0) or (c & top and (c ^ round_number ^ 1) & 1 == 0)
    ]


def half_size(blocks):
    return 1 << (blocks.bit_length() // 2 - 1)


def multiply_kernel(half, root, role_ref, *refs):
    shards, (send_ref, keep_ref) = refs[:-2], refs[-2:]
    own, across = shards[0], shards[1:half]
    crossed, passed = shards[half : 2 * half], shards[2 * half :]
    rows = own.shape[0]

    def product(first, second):
        dims = (((1,), (1,)), ((), ()))
        out = lax.dot_general(first, second, dims, preferred_element_type=jnp.float32)
        return (out / root).astype(jnp.bfloat16)

    def stacked(parts):
        return jnp.concatenate([part[...] for part in parts], axis=0)

    def store(lefts, rights, left_ref, right_ref):
        left_all, right_all = stacked(lefts), stacked(rights)
        by_left = product(left_all, right_all)
        by_right = product(right_all, left_all)
        for t in range(half):
            left_ref[t] = by_left[t * rows : (t + 1) * rows]
            right_ref[t] = by_right[t * rows : (t + 1) * rows]

    @pl.when(role_ref[0] == 1)
    def _():
        rights = (crossed[1], crossed[0]) + crossed[2:]
        store((own,) + across, rights, keep_ref, send_ref)

    @pl.when(role_ref[0] == 0)
    def _():
        store(crossed, (across[0],) + passed, send_ref, keep_ref)


def multiply(role, half, own, across, crossed, passed):
    rows, markers = own.shape
    shards = [own, *across, *crossed, *passed]
    vmem = pl.BlockSpec(memory_space=pltpu.VMEM)
    block = jax.ShapeDtypeStruct((half, rows, half * rows), jnp.bfloat16)
    return pl.pallas_call(
        functools.partial(multiply_kernel, half, math.sqrt(markers)),
        out_shape=(block, block),
        in_specs=[pl.BlockSpec(memory_space=pltpu.SMEM)] + [vmem] * len(shards),
        out_specs=(vmem, vmem),
        compiler_params=pltpu.CompilerParams(vmem_limit_bytes=VMEM_BYTES),
    )(role, *shards)


def place_kernel(half, role_ref, *refs):
    parts, out_ref = refs[:-1], refs[-1]
    rows = out_ref.shape[1]
    near = 2 * half

    def put(offset, value):
        block = jnp.bitwise_xor(role_ref[1], offset)
        out_ref[0, :, pl.ds(pl.multiple_of(block * rows, rows), rows)] = value

    @pl.when(role_ref[0] == 1)
    def _():
        for t in range(half):
            for odd in range(2):
                for m in range(half):
                    put(2 * t + odd + near * m, parts[t][odd, :, m * rows : (m + 1) * rows])

    @pl.when(role_ref[0] == 0)
    def _():
        for t in range(half):
            for even in range(2):
                for s in range(half):
                    put(2 * s + 1 - even + near * t, parts[t][even, :, s * rows : (s + 1) * rows])


def place_blocks(role, half, parts):
    rows = parts[0].shape[1]
    vmem = pl.BlockSpec(memory_space=pltpu.VMEM)
    return pl.pallas_call(
        functools.partial(place_kernel, half),
        out_shape=jax.ShapeDtypeStruct((1, rows, 2 * half * half * rows), jnp.bfloat16),
        in_specs=[pl.BlockSpec(memory_space=pltpu.SMEM)] + [vmem] * len(parts),
        out_specs=vmem,
        compiler_params=pltpu.CompilerParams(vmem_limit_bytes=VMEM_BYTES),
    )(role, *parts)


def one_round(round_number, cohorts, blocks, own):
    half = half_size(blocks)
    near = 2 * half
    left = left_cohorts(cohorts, round_number)

    def send(value, *legs):
        pairs = []
        for c in left:
            for i in range(blocks):
                for leg in legs:
                    (c0, i0), (c1, i1) = leg(c, i)
                    pairs.append((c0 * blocks + i0, c1 * blocks + i1))
        return lax.ppermute(value, AXES, pairs)

    def left_to_left(d):
        return lambda c, i: ((c, i), (c, i ^ d))

    def left_to_mate(d):
        return lambda c, i: ((c, i), (c ^ 1, i ^ d))

    def mate_to_left(d):
        return lambda c, i: ((c ^ 1, i), (c, i ^ d))

    def mate_to_mate(c, i):
        return (c ^ 1, i), (c ^ 1, i)

    def owner_to_left(d):
        return lambda c, i: ((c ^ round_number, i ^ d), (c, i))

    def owner_to_mate(d):
        return lambda c, i: ((c ^ round_number, i ^ d), (c ^ 1, i))

    def mate_to_owner(d):
        return lambda c, i: ((c ^ 1, i), (c ^ round_number, i ^ d))

    cohort = lax.axis_index("cohort")
    is_left = functools.reduce(jnp.logical_or, [cohort == c for c in left])
    role = jnp.stack([is_left.astype(jnp.int32), lax.axis_index("person")])

    across = [send(own, left_to_left(2), owner_to_mate(0))]
    crossed = [send(own, left_to_mate(1), owner_to_left(near))]
    for t in range(2, half):
        across.append(send(own, left_to_left(2 * t), mate_to_mate))
    crossed.append(send(across[0], left_to_mate(1), mate_to_left(0)))
    for t in range(2, half):
        value = jnp.where(is_left, across[t - 1], own)
        crossed.append(send(value, left_to_mate(1), owner_to_left(near * t)))
    passed = [
        send(crossed[0 if m == 1 else m], left_to_mate(0), mate_to_left(0))
        for m in range(1, half)
    ]
    sent, kept = multiply(role, half, own, across, crossed, passed)
    got = send(sent, mate_to_left(1), left_to_mate(0))
    parts = [jnp.stack([kept[t], got[t]]) for t in range(half)]
    for t in range(half):
        if t or round_number != 1:
            parts[t] = send(parts[t], left_to_left(2 * t), mate_to_owner(near * t))
    return place_blocks(role, half, parts)


def standard_rows(rows, counts, people_all):
    totals = lax.psum(counts, "person")
    freq = (totals.astype(jnp.float32) + 1.0) / (2.0 * people_all + 2.0)
    scale = 1.0 / jnp.sqrt(2.0 * freq * (1.0 - freq))
    return ((rows.astype(jnp.float32) - 2.0 * freq) * scale).astype(jnp.bfloat16)


def on_device(dosages, allele_counts, partner):
    cohorts, blocks = lax.axis_size("cohort"), lax.axis_size("person")
    own = standard_rows(dosages[0], allele_counts[0], dosages.shape[1] * blocks)
    rounds = [
        functools.partial(one_round, round_number, cohorts, blocks)
        for round_number in range(1, cohorts)
    ]
    return lax.switch(partner[0] - 1, rounds, own)


def solution(mesh):
    placed = (P("cohort", "person", None), P("cohort", "person", None), P())
    return jax.shard_map(
        on_device,
        mesh=mesh,
        in_specs=placed,
        out_specs=P("cohort", "person", None),
        check_vma=False,
    )
```

```python
import functools
import math

import jax
import jax.numpy as jnp
from jax import lax
from jax.experimental import pallas as pl
from jax.experimental.pallas import tpu as pltpu
from jax.sharding import PartitionSpec as P

AXES = ("cohort", "person")
VMEM_BYTES = 48 * 1024 * 1024


def left_cohorts(cohorts, round_number):
    if round_number == 1:
        return [c for c in range(cohorts) if c & 1 == 0]
    top = 1 << (round_number.bit_length() - 1)
    return [
        c
        for c in range(cohorts)
        if (c & top == 0 and c & 1 == 0) or (c & top and (c ^ round_number ^ 1) & 1 == 0)
    ]


def half_size(blocks):
    return 1 << (blocks.bit_length() // 2 - 1)


def far_step(half, m):
    return 2 * half * m + half * (m & 1)


def flipped(half, place):
    low, high = half.bit_length() - 1, half.bit_length()
    return ((place >> low) ^ (place >> high)) & 1


def standard_kernel(people_all, *refs):
    counts, rows_ref, out_ref = refs[:-2], refs[-2], refs[-1]
    totals = counts[0][...]
    for part in counts[1:]:
        totals = totals + part[...]
    freq = (totals.astype(jnp.float32) + 1.0) / (2.0 * people_all + 2.0)
    scale = 1.0 / jnp.sqrt(2.0 * freq * (1.0 - freq))
    rows = rows_ref[...].astype(jnp.float32)
    out_ref[...] = ((rows - 2.0 * freq) * scale).astype(jnp.bfloat16)


def standard_rows(rows, counts, people_all):
    vmem = pl.BlockSpec(memory_space=pltpu.VMEM)
    return pl.pallas_call(
        functools.partial(standard_kernel, people_all),
        out_shape=jax.ShapeDtypeStruct(rows.shape, jnp.bfloat16),
        in_specs=[vmem] * (len(counts) + 1),
        out_specs=vmem,
        compiler_params=pltpu.CompilerParams(vmem_limit_bytes=VMEM_BYTES),
    )(*counts, rows)


def multiply_kernel(half, root, role_ref, *refs):
    shards, send_ref, keep_ref = refs[: 3 * half], refs[3 * half : 4 * half], refs[4 * half :]
    across = shards[:half]
    fetched, passed = shards[half : 2 * half], shards[2 * half :]
    rows = across[0].shape[0]

    def product(first, second):
        dims = (((1,), (1,)), ((), ()))
        out = lax.dot_general(first, second, dims, preferred_element_type=jnp.float32)
        return (out / root).astype(jnp.bfloat16)

    def store(lefts, rights, left_ref, right_ref):
        left_all = jnp.concatenate([part[...] for part in lefts], axis=0)
        right_all = jnp.concatenate([part[...] for part in rights], axis=0)
        by_left = product(left_all, right_all)
        by_right = product(right_all, left_all)
        for t in range(half):
            left_ref[t][...] = by_left[t * rows : (t + 1) * rows]
            right_ref[t][...] = by_right[t * rows : (t + 1) * rows]

    @pl.when(role_ref[0] == 1)
    def _():
        store(across, fetched, keep_ref, send_ref)

    @pl.when(role_ref[0] == 0)
    def _():
        store(fetched, passed, send_ref, keep_ref)


def multiply(role, half, across, fetched, passed):
    rows, markers = across[0].shape
    shards = [*across, *fetched, *passed]
    vmem = pl.BlockSpec(memory_space=pltpu.VMEM)
    block = jax.ShapeDtypeStruct((rows, half * rows), jnp.bfloat16)
    outs = pl.pallas_call(
        functools.partial(multiply_kernel, half, math.sqrt(markers)),
        out_shape=[block] * (2 * half),
        in_specs=[pl.BlockSpec(memory_space=pltpu.SMEM)] + [vmem] * len(shards),
        out_specs=[vmem] * (2 * half),
        compiler_params=pltpu.CompilerParams(vmem_limit_bytes=VMEM_BYTES),
    )(role, *shards)
    return outs[:half], outs[half:]


def place_kernel(half, role_ref, *refs):
    sent, kept, out_ref = refs[:half], refs[half:-1], refs[-1]
    rows = out_ref.shape[1]
    place = role_ref[1]
    flip = flipped(half, place)

    def put(block, value):
        out_ref[0, :, pl.ds(pl.multiple_of(block * rows, rows), rows)] = value

    @pl.when(role_ref[0] == 1)
    def _():
        for t in range(half):
            for part, chip in ((kept[t], place ^ 2 * t), (sent[t], place ^ 2 * t + 1)):
                turn = flipped(half, chip)
                for m in range(half):
                    put(chip ^ far_step(half, m ^ turn), part[:, m * rows : (m + 1) * rows])

    @pl.when(role_ref[0] == 0)
    def _():
        for t in range(half):
            chip = place ^ far_step(half, t ^ flip)
            for d in range(half):
                put(chip ^ 2 * d, sent[t][:, d * rows : (d + 1) * rows])
                put(chip ^ 2 * d + 1, kept[t][:, d * rows : (d + 1) * rows])


def place_blocks(role, half, sent, kept):
    rows = sent[0].shape[0]
    vmem = pl.BlockSpec(memory_space=pltpu.VMEM)
    return pl.pallas_call(
        functools.partial(place_kernel, half),
        out_shape=jax.ShapeDtypeStruct((1, rows, 2 * half * half * rows), jnp.bfloat16),
        in_specs=[pl.BlockSpec(memory_space=pltpu.SMEM)] + [vmem] * (2 * half),
        out_specs=vmem,
        compiler_params=pltpu.CompilerParams(vmem_limit_bytes=VMEM_BYTES),
    )(role, *sent, *kept)


def one_round(round_number, cohorts, blocks, own):
    half = half_size(blocks)
    left = left_cohorts(cohorts, round_number)

    def send(value, *legs):
        pairs = []
        for c in left:
            for i in range(blocks):
                for leg in legs:
                    (c0, i0), (c1, i1) = leg(c, i)
                    pairs.append((c0 * blocks + i0, c1 * blocks + i1))
        return lax.ppermute(value, AXES, pairs)

    def right(i, t):
        return i ^ far_step(half, t ^ flipped(half, i))

    def left_to_left(d):
        return lambda c, i: ((c, i), (c, i ^ d))

    def left_to_mate(d):
        return lambda c, i: ((c, i), (c ^ 1, i ^ d))

    def mate_to_left(d):
        return lambda c, i: ((c ^ 1, i), (c, i ^ d))

    def mate_to_mate(c, i):
        return (c ^ 1, i), (c ^ 1, i)

    def owner_to_left(t):
        return lambda c, i: ((c ^ round_number, right(i, t)), (c, i))

    def left_to_owner(t):
        return lambda c, i: ((c, i), (c ^ round_number, right(i, t)))

    def mate_to_owner(t):
        return lambda c, i: ((c ^ 1, i), (c ^ round_number, right(i, t)))

    cohort = lax.axis_index("cohort")
    is_left = functools.reduce(jnp.logical_or, [cohort == c for c in left])
    role = jnp.stack([is_left.astype(jnp.int32), lax.axis_index("person")])

    across = [own] + [send(own, left_to_left(2 * t), mate_to_mate) for t in range(1, half)]
    fetched = [send(across[t], left_to_mate(1), owner_to_left(t)) for t in range(half)]
    passed = [send(fetched[t], left_to_mate(0), mate_to_left(0)) for t in range(half)]
    sent, kept = multiply(role, half, across, fetched, passed)
    sent, kept = list(sent), list(kept)
    for t in reversed(range(half)):
        sent[t] = send(sent[t], mate_to_left(2 * t + 1), left_to_owner(t))
        kept[t] = send(kept[t], left_to_left(2 * t), mate_to_owner(t))
    return place_blocks(role, half, sent, kept)


def on_device(dosages, allele_counts, partner):
    cohorts, blocks = lax.axis_size("cohort"), lax.axis_size("person")
    half = half_size(blocks)

    def swap(value, step):
        return lax.ppermute(value, "person", [(i, i ^ step) for i in range(blocks)])

    near = allele_counts[0]
    for step in range(1, 2 * half):
        near = near + swap(allele_counts[0], step)
    counts = [near] + [swap(near, far_step(half, m)) for m in range(1, half)]
    own = standard_rows(dosages[0], counts, dosages.shape[1] * blocks)
    rounds = [
        functools.partial(one_round, round_number, cohorts, blocks)
        for round_number in range(1, cohorts)
    ]
    return lax.switch(partner[0] - 1, rounds, own)


def solution(mesh):
    placed = (P("cohort", "person", None), P("cohort", "person", None), P())
    return jax.shard_map(
        on_device,
        mesh=mesh,
        in_specs=placed,
        out_specs=P("cohort", "person", None),
        check_vma=False,
    )
```

```python
import functools
import math

import jax
import jax.numpy as jnp
from jax import lax
from jax.experimental import pallas as pl
from jax.experimental.pallas import tpu as pltpu
from jax.sharding import PartitionSpec as P

AXES = ("cohort", "person")
VMEM_BYTES = 48 * 1024 * 1024


def left_cohorts(cohorts, round_number):
    if round_number == 1:
        return [c for c in range(cohorts) if c & 1 == 0]
    top = 1 << (round_number.bit_length() - 1)
    return [
        c
        for c in range(cohorts)
        if (c & top == 0 and c & 1 == 0) or (c & top and (c ^ round_number ^ 1) & 1 == 0)
    ]


def half_size(blocks):
    return 1 << (blocks.bit_length() // 2 - 1)


def far_step(half, m):
    return 2 * half * m + half * (m & 1)


def flipped(half, place):
    low, high = half.bit_length() - 1, half.bit_length()
    return 1 ^ ((place >> low) ^ (place >> high)) & 1


def load_kernel(rows_ref, out_ref, sem):
    copy = pltpu.make_async_copy(rows_ref, out_ref, sem)
    copy.start()
    copy.wait()


def load_rows(rows):
    return pl.pallas_call(
        load_kernel,
        out_shape=jax.ShapeDtypeStruct(rows.shape, rows.dtype),
        in_specs=[pl.BlockSpec(memory_space=pltpu.HBM)],
        out_specs=pl.BlockSpec(memory_space=pltpu.VMEM),
        scratch_shapes=[pltpu.SemaphoreType.DMA],
        compiler_params=pltpu.CompilerParams(vmem_limit_bytes=VMEM_BYTES),
    )(rows)


def sum_kernel(*refs):
    total = refs[0][...]
    for ref in refs[1:-1]:
        total = total + ref[...]
    refs[-1][...] = total


def sum_of(parts):
    vmem = pl.BlockSpec(memory_space=pltpu.VMEM)
    return pl.pallas_call(
        sum_kernel,
        out_shape=jax.ShapeDtypeStruct(parts[0].shape, parts[0].dtype),
        in_specs=[vmem] * len(parts),
        out_specs=vmem,
        compiler_params=pltpu.CompilerParams(vmem_limit_bytes=VMEM_BYTES),
    )(*parts)


def multiply_kernel(half, people_all, role_ref, *refs):
    groups = [refs[n * half : (n + 1) * half] for n in range(7)]
    first, second, third, direct, crossed, send_ref, keep_ref = groups
    rows, markers = first[0].shape
    root = math.sqrt(markers)

    def standard(parts, counts):
        totals = counts[0][...]
        for part in counts[1:]:
            totals = totals + part[...]
        freq = (totals.astype(jnp.float32) + 1.0) / (2.0 * people_all + 2.0)
        scale = 1.0 / jnp.sqrt(2.0 * freq * (1.0 - freq))
        whole = jnp.concatenate([part[...] for part in parts], axis=0)
        return ((whole.astype(jnp.float32) - 2.0 * freq) * scale).astype(jnp.bfloat16)

    def product(one, other):
        dims = (((1,), (1,)), ((), ()))
        out = lax.dot_general(one, other, dims, preferred_element_type=jnp.float32)
        return (out / root).astype(jnp.bfloat16)

    def store(lefts, left_counts, rights, right_counts, left_ref, right_ref):
        left_all = standard(lefts, left_counts)
        right_all = standard(rights, right_counts)
        by_left = product(left_all, right_all)
        by_right = product(right_all, left_all)
        for t in range(half):
            left_ref[t][...] = by_left[t * rows : (t + 1) * rows]
            right_ref[t][...] = by_right[t * rows : (t + 1) * rows]

    @pl.when(role_ref[0] == 1)
    def _():
        store(first, direct, second, crossed, keep_ref, send_ref)

    @pl.when(role_ref[0] == 0)
    def _():
        store(second, crossed, third[:1] + first[1:], direct, send_ref, keep_ref)


def multiply(role, half, people_all, *groups):
    shards = [array for group in groups for array in group]
    rows = shards[0].shape[0]
    vmem = pl.BlockSpec(memory_space=pltpu.VMEM)
    block = jax.ShapeDtypeStruct((rows, half * rows), jnp.bfloat16)
    outs = pl.pallas_call(
        functools.partial(multiply_kernel, half, people_all),
        out_shape=[block] * (2 * half),
        in_specs=[pl.BlockSpec(memory_space=pltpu.SMEM)] + [vmem] * len(shards),
        out_specs=[vmem] * (2 * half),
        compiler_params=pltpu.CompilerParams(vmem_limit_bytes=VMEM_BYTES),
    )(role, *shards)
    return list(outs[:half]), list(outs[half:])


def place_kernel(half, role_ref, *refs):
    sent, kept, out_ref = refs[:half], refs[half:-1], refs[-1]
    rows = out_ref.shape[1]
    place = role_ref[1]
    flip = flipped(half, place)

    def put(block, value):
        out_ref[0, :, pl.ds(pl.multiple_of(block * rows, rows), rows)] = value

    @pl.when(role_ref[0] == 1)
    def _():
        for t in range(half):
            for part, chip in ((kept[t], place ^ 2 * t), (sent[t], place ^ 2 * t + 1)):
                turn = flipped(half, chip)
                for m in range(half):
                    put(chip ^ far_step(half, m ^ turn), part[:, m * rows : (m + 1) * rows])

    @pl.when(role_ref[0] == 0)
    def _():
        for t in range(half):
            chip = place ^ far_step(half, t ^ flip)
            for d in range(half):
                put(chip ^ 2 * d, sent[t][:, d * rows : (d + 1) * rows])
                put(chip ^ 2 * d + 1, kept[t][:, d * rows : (d + 1) * rows])


def place_blocks(role, half, sent, kept):
    rows = sent[0].shape[0]
    vmem = pl.BlockSpec(memory_space=pltpu.VMEM)
    return pl.pallas_call(
        functools.partial(place_kernel, half),
        out_shape=jax.ShapeDtypeStruct((1, rows, 2 * half * half * rows), jnp.bfloat16),
        in_specs=[pl.BlockSpec(memory_space=pltpu.SMEM)] + [vmem] * (2 * half),
        out_specs=vmem,
        compiler_params=pltpu.CompilerParams(vmem_limit_bytes=VMEM_BYTES),
    )(role, *sent, *kept)


def one_round(round_number, cohorts, blocks, own, beside, near_counts):
    half = half_size(blocks)
    left = left_cohorts(cohorts, round_number)

    def send(value, *legs):
        pairs = []
        for c in left:
            for i in range(blocks):
                for leg in legs:
                    (c0, i0), (c1, i1) = leg(c, i)
                    pairs.append((c0 * blocks + i0, c1 * blocks + i1))
        return lax.ppermute(value, AXES, pairs)

    def right(i, t):
        return i ^ far_step(half, t ^ flipped(half, i))

    def left_to_left(d):
        return lambda c, i: ((c, i), (c, i ^ d))

    def left_to_mate(d):
        return lambda c, i: ((c, i), (c ^ 1, i ^ d))

    def mate_to_left(d):
        return lambda c, i: ((c ^ 1, i), (c, i ^ d))

    def mate_to_mate(d):
        return lambda c, i: ((c ^ 1, i), (c ^ 1, i ^ d))

    def owner_to_left(d):
        return lambda c, i: ((c ^ round_number, i), (c, i ^ d))

    def owner_to_mate(d):
        return lambda c, i: ((c ^ round_number, i), (c ^ 1, i ^ d))

    def right_rows_to_mate(t):
        return lambda c, i: ((c ^ 1, i), (c ^ round_number, right(i, t)))

    def right_rows_to_left(t):
        return lambda c, i: ((c, i), (c ^ 1 ^ round_number, right(i, t)))

    def left_to_owner(t):
        return lambda c, i: ((c, i), (c ^ round_number, right(i, t)))

    def mate_to_owner(t):
        return lambda c, i: ((c ^ 1, i), (c ^ round_number, right(i, t)))

    cohort = lax.axis_index("cohort")
    is_left = functools.reduce(jnp.logical_or, [cohort == c for c in left])
    role = jnp.stack([is_left.astype(jnp.int32), lax.axis_index("person")])

    first = [own] + [
        send(own, left_to_left(2 * t), right_rows_to_mate(t)) for t in range(1, half)
    ]
    second = [send(beside, right_rows_to_left(0), mate_to_mate(1))]
    direct, crossed = [], []
    for m in range(half):
        d = far_step(half, m)
        direct.append(send(near_counts, left_to_left(d), owner_to_mate(d)))
        crossed.append(send(near_counts, left_to_mate(d), owner_to_left(d)))
    third = [send(second[0], left_to_mate(0), mate_to_left(0))]
    third += [send(first[t], left_to_mate(1), mate_to_left(0)) for t in range(1, half)]
    second += third[1:]
    people_all = own.shape[0] * blocks
    sent, kept = multiply(role, half, people_all, first, second, third, direct, crossed)
    for t in reversed(range(half)):
        sent[t] = send(sent[t], mate_to_left(2 * t + 1), left_to_owner(t))
        kept[t] = send(kept[t], left_to_left(2 * t), mate_to_owner(t))
    return place_blocks(role, half, sent, kept)


def on_device(dosages, allele_counts, partner):
    cohorts, blocks = lax.axis_size("cohort"), lax.axis_size("person")
    counts = allele_counts[0]
    near = [counts]
    for step in range(1, 2 * half_size(blocks)):
        near.append(lax.ppermute(counts, "person", [(i, i ^ step) for i in range(blocks)]))
    own = load_rows(dosages[0])
    beside = lax.ppermute(own, "cohort", [(c, c ^ 1) for c in range(cohorts)])
    near_counts = sum_of(near)
    rounds = [
        functools.partial(one_round, round_number, cohorts, blocks)
        for round_number in range(1, cohorts)
    ]
    return lax.switch(partner[0] - 1, rounds, own, beside, near_counts)


def solution(mesh):
    placed = (P("cohort", "person", None), P("cohort", "person", None), P())
    return jax.shard_map(
        on_device,
        mesh=mesh,
        in_specs=placed,
        out_specs=P("cohort", "person", None),
        check_vma=False,
    )
```

```python
import functools
import math

import jax
import jax.numpy as jnp
from jax import lax
from jax.experimental import pallas as pl
from jax.experimental.pallas import tpu as pltpu
from jax.sharding import PartitionSpec as P

AXES = ("cohort", "person")
VMEM_BYTES = 48 * 1024 * 1024


def left_cohorts(cohorts, round_number):
    if round_number == 1:
        return [c for c in range(cohorts) if c & 1 == 0]
    top = 1 << (round_number.bit_length() - 1)
    return [
        c
        for c in range(cohorts)
        if (c & top == 0 and c & 1 == 0) or (c & top and (c ^ round_number ^ 1) & 1 == 0)
    ]


def half_size(blocks):
    return 1 << (blocks.bit_length() // 2 - 1)


def load_kernel(rows_ref, out_ref, sem):
    copy = pltpu.make_async_copy(rows_ref, out_ref, sem)
    copy.start()
    copy.wait()


def load_rows(rows):
    return pl.pallas_call(
        load_kernel,
        out_shape=jax.ShapeDtypeStruct(rows.shape, rows.dtype),
        in_specs=[pl.BlockSpec(memory_space=pltpu.HBM)],
        out_specs=pl.BlockSpec(memory_space=pltpu.VMEM),
        scratch_shapes=[pltpu.SemaphoreType.DMA],
        compiler_params=pltpu.CompilerParams(vmem_limit_bytes=VMEM_BYTES),
    )(rows)


def sum_kernel(parts_ref, out_ref):
    total = parts_ref[0]
    for n in range(1, parts_ref.shape[0]):
        total = total + parts_ref[n]
    out_ref[...] = total


def sum_of(parts):
    vmem = pl.BlockSpec(memory_space=pltpu.VMEM)
    return pl.pallas_call(
        sum_kernel,
        out_shape=jax.ShapeDtypeStruct(parts.shape[1:], parts.dtype),
        in_specs=[vmem],
        out_specs=vmem,
        compiler_params=pltpu.CompilerParams(vmem_limit_bytes=VMEM_BYTES),
    )(parts)


def multiply_kernel(half, people_all, role_ref, *refs):
    groups = [refs[n * half : (n + 1) * half] for n in range(3)]
    first, second, third = groups
    direct, crossed = refs[3 * half : 3 * half + 2]
    send_ref, keep_ref = refs[3 * half + 2 : 4 * half + 2], refs[4 * half + 2 :]
    rows, markers = first[0].shape
    root = math.sqrt(markers)

    def standard(parts, totals):
        freq = (totals[...].astype(jnp.float32) + 1.0) / (2.0 * people_all + 2.0)
        scale = 1.0 / jnp.sqrt(2.0 * freq * (1.0 - freq))
        whole = jnp.concatenate([part[...] for part in parts], axis=0)
        return ((whole.astype(jnp.float32) - 2.0 * freq) * scale).astype(jnp.bfloat16)

    def product(one, other):
        dims = (((1,), (1,)), ((), ()))
        out = lax.dot_general(one, other, dims, preferred_element_type=jnp.float32)
        return (out / root).astype(jnp.bfloat16)

    def store(lefts, left_totals, rights, right_totals, left_ref, right_ref):
        left_all = standard(lefts, left_totals)
        right_all = standard(rights, right_totals)
        by_left = product(left_all, right_all)
        by_right = product(right_all, left_all)
        for t in range(half):
            left_ref[t][...] = by_left[t * rows : (t + 1) * rows]
            right_ref[t][...] = by_right[t * rows : (t + 1) * rows]

    @pl.when(role_ref[0] == 1)
    def _():
        store(first, direct, second, crossed, keep_ref, send_ref)

    @pl.when(role_ref[0] == 0)
    def _():
        store(second, crossed, third[:1] + first[1:], direct, send_ref, keep_ref)


def multiply(role, people_all, first, second, third, direct, crossed):
    half = len(first)
    shards = [*first, *second, *third, direct, crossed]
    rows = shards[0].shape[0]
    vmem = pl.BlockSpec(memory_space=pltpu.VMEM)
    block = jax.ShapeDtypeStruct((rows, half * rows), jnp.bfloat16)
    outs = pl.pallas_call(
        functools.partial(multiply_kernel, half, people_all),
        out_shape=[block] * (2 * half),
        in_specs=[pl.BlockSpec(memory_space=pltpu.SMEM)] + [vmem] * len(shards),
        out_specs=[vmem] * (2 * half),
        compiler_params=pltpu.CompilerParams(vmem_limit_bytes=VMEM_BYTES),
    )(role, *shards)
    return list(outs[:half]), list(outs[half:])


def place_kernel(half, role_ref, *refs):
    sent, kept, out_ref = refs[:half], refs[half:-1], refs[-1]
    rows = out_ref.shape[1]
    place = role_ref[1]
    near = 2 * half

    def put(block, value):
        out_ref[0, :, pl.ds(pl.multiple_of(block * rows, rows), rows)] = value

    @pl.when(role_ref[0] == 1)
    def _():
        for t in range(half):
            for part, chip in ((kept[t], place ^ 2 * t), (sent[t], place ^ 2 * t + 1)):
                for m in range(half):
                    put(chip ^ near * m, part[:, m * rows : (m + 1) * rows])

    @pl.when(role_ref[0] == 0)
    def _():
        for t in range(half):
            chip = place ^ near * t
            for d in range(half):
                put(chip ^ 2 * d, sent[t][:, d * rows : (d + 1) * rows])
                put(chip ^ 2 * d + 1, kept[t][:, d * rows : (d + 1) * rows])


def place_blocks(role, half, sent, kept):
    rows = sent[0].shape[0]
    vmem = pl.BlockSpec(memory_space=pltpu.VMEM)
    return pl.pallas_call(
        functools.partial(place_kernel, half),
        out_shape=jax.ShapeDtypeStruct((1, rows, 2 * half * half * rows), jnp.bfloat16),
        in_specs=[pl.BlockSpec(memory_space=pltpu.SMEM)] + [vmem] * (2 * half),
        out_specs=vmem,
        compiler_params=pltpu.CompilerParams(vmem_limit_bytes=VMEM_BYTES),
    )(role, *sent, *kept)


def one_round(round_number, cohorts, blocks, own, counts):
    half = half_size(blocks)
    near = 2 * half
    left = left_cohorts(cohorts, round_number)

    def send(value, *legs):
        pairs = []
        for c in left:
            for i in range(blocks):
                for leg in legs:
                    (c0, i0), (c1, i1) = leg(c, i)
                    pairs.append((c0 * blocks + i0, c1 * blocks + i1))
        return lax.ppermute(value, AXES, pairs)

    def left_to_left(d):
        return lambda c, i: ((c, i), (c, i ^ d))

    def left_to_mate(d):
        return lambda c, i: ((c, i), (c ^ 1, i ^ d))

    def mate_to_left(d):
        return lambda c, i: ((c ^ 1, i), (c, i ^ d))

    def mate_to_mate(d):
        return lambda c, i: ((c ^ 1, i), (c ^ 1, i ^ d))

    def owner_to_left(c, i):
        return (c ^ round_number, i), (c, i)

    def owner_to_mate(c, i):
        return (c ^ round_number, i), (c ^ 1, i)

    def right_rows_to_mate(t):
        return lambda c, i: ((c ^ 1, i), (c ^ round_number, i ^ near * t))

    def right_rows_to_left(c, i):
        return (c, i), (c ^ 1 ^ round_number, i)

    def left_to_owner(t):
        return lambda c, i: ((c, i), (c ^ round_number, i ^ near * t))

    def mate_to_owner(t):
        return lambda c, i: ((c ^ 1, i), (c ^ round_number, i ^ near * t))

    cohort = lax.axis_index("cohort")
    is_left = functools.reduce(jnp.logical_or, [cohort == c for c in left])
    role = jnp.stack([is_left.astype(jnp.int32), lax.axis_index("person")])

    first = [own] + [
        send(own, left_to_left(2 * t), right_rows_to_mate(t)) for t in range(1, half)
    ]
    beside = send(own, left_to_mate(0), mate_to_left(0))
    second = [send(beside, right_rows_to_left, mate_to_mate(1))]
    counts, _ = lax.optimization_barrier((counts, beside))
    spread = jnp.broadcast_to(counts[None], (blocks, *counts.shape))
    totals = sum_of(lax.all_to_all(spread, "person", 0, 0, tiled=True))
    *first[1:], totals = lax.optimization_barrier((*first[1:], totals))
    crossed = send(totals, left_to_mate(0), owner_to_left)
    direct = totals
    if round_number != 1:
        direct = send(totals, left_to_left(0), owner_to_mate)
    third = [send(second[0], left_to_mate(0), mate_to_left(0))]
    third += [send(first[t], left_to_mate(1), mate_to_left(0)) for t in range(1, half)]
    second += third[1:]
    people_all = own.shape[0] * blocks
    sent, kept = multiply(role, people_all, first, second, third, direct, crossed)
    for t in reversed(range(half)):
        sent[t] = send(sent[t], mate_to_left(2 * t + 1), left_to_owner(t))
        if t or round_number != 1:
            kept[t] = send(kept[t], left_to_left(2 * t), mate_to_owner(t))
    return place_blocks(role, half, sent, kept)


def on_device(dosages, allele_counts, partner):
    cohorts, blocks = lax.axis_size("cohort"), lax.axis_size("person")
    rounds = [
        functools.partial(one_round, round_number, cohorts, blocks)
        for round_number in range(1, cohorts)
    ]
    own = load_rows(dosages[0])
    return lax.switch(partner[0] - 1, rounds, own, allele_counts[0])


def solution(mesh):
    placed = (P("cohort", "person", None), P("cohort", "person", None), P())
    return jax.shard_map(
        on_device,
        mesh=mesh,
        in_specs=placed,
        out_specs=P("cohort", "person", None),
        check_vma=False,
    )
```

```python
import functools
import math

import jax
import jax.numpy as jnp
from jax import lax
from jax.experimental import pallas as pl
from jax.experimental.pallas import tpu as pltpu
from jax.sharding import PartitionSpec as P

AXES = ("cohort", "person")
VMEM_BYTES = 48 * 1024 * 1024
VMEM_WHOLE = 64 * 1024 * 1024
VMEM_ROOM = 128 * 1024


def left_cohorts(cohorts, round_number):
    if round_number == 1:
        return [c for c in range(cohorts) if c & 1 == 0]
    top = 1 << (round_number.bit_length() - 1)
    return [
        c
        for c in range(cohorts)
        if (c & top == 0 and c & 1 == 0) or (c & top and (c ^ round_number ^ 1) & 1 == 0)
    ]


def half_size(blocks):
    return 1 << (blocks.bit_length() // 2 - 1)


def load_kernel(partner_ref, counts_ref, rows_ref, index_ref, spread_ref, out_ref, first, sems):
    copies = [
        pltpu.make_async_copy(rows_ref, out_ref, sems.at[0]),
        pltpu.make_async_copy(counts_ref, spread_ref.at[0], sems.at[1]),
        pltpu.make_async_copy(partner_ref, first, sems.at[2]),
    ]
    for copy in copies:
        copy.start()
    for copy in copies[1:]:
        copy.wait()
    index_ref[0] = first[0] - 1
    for n in range(1, spread_ref.shape[0]):
        spread_ref[n] = spread_ref[0]
    copies[0].wait()


def load(partner, counts, rows, blocks):
    vmem, smem = (pl.BlockSpec(memory_space=space) for space in (pltpu.VMEM, pltpu.SMEM))
    held = rows.size * rows.dtype.itemsize + blocks * counts.size * counts.dtype.itemsize
    return pl.pallas_call(
        load_kernel,
        out_shape=(
            jax.ShapeDtypeStruct((1,), jnp.int32),
            jax.ShapeDtypeStruct((blocks, *counts.shape), counts.dtype),
            jax.ShapeDtypeStruct(rows.shape, rows.dtype),
        ),
        in_specs=[pl.BlockSpec(memory_space=pl.ANY)] * 3,
        out_specs=(smem, vmem, vmem),
        scratch_shapes=[pltpu.SMEM(partner.shape, jnp.int32), pltpu.SemaphoreType.DMA((3,))],
        compiler_params=pltpu.CompilerParams(vmem_limit_bytes=VMEM_WHOLE - VMEM_ROOM - held),
    )(partner, counts, rows)


def sum_kernel(parts_ref, out_ref):
    total = parts_ref[0]
    for n in range(1, parts_ref.shape[0]):
        total = total + parts_ref[n]
    out_ref[...] = total


def sum_of(parts):
    vmem = pl.BlockSpec(memory_space=pltpu.VMEM)
    return pl.pallas_call(
        sum_kernel,
        out_shape=jax.ShapeDtypeStruct(parts.shape[1:], parts.dtype),
        in_specs=[vmem],
        out_specs=vmem,
        compiler_params=pltpu.CompilerParams(vmem_limit_bytes=VMEM_BYTES),
    )(parts)


def standard_rows(rows, totals, people_all):
    freq = (totals.astype(jnp.float32) + 1.0) / (2.0 * people_all + 2.0)
    scale = 1.0 / jnp.sqrt(2.0 * freq * (1.0 - freq))
    return ((rows.astype(jnp.float32) - 2.0 * freq) * scale).astype(jnp.bfloat16)


def scaled_product(one, other):
    dims = (((1,), (1,)), ((), ()))
    out = lax.dot_general(one, other, dims, preferred_element_type=jnp.float32)
    return (out / math.sqrt(one.shape[1])).astype(jnp.bfloat16)


def early_kernel(half, people_all, role_ref, *refs):
    own_ref, passed_ref, single_ref, direct_ref, crossed_ref = refs[:5]
    across, (wide_ref, std_ref, sent_ref) = refs[5:-3], refs[-3:]
    rows = own_ref.shape[0]
    direct, crossed = direct_ref[...], crossed_ref[...]

    @pl.when(role_ref[0] == 1)
    def _():
        wide_ref[:rows, :] = standard_rows(own_ref[...], direct, people_all)

    @pl.when(role_ref[0] == 0)
    def _():
        wide_ref[:rows, :] = standard_rows(passed_ref[...], direct, people_all)

    for t in range(1, half):
        wide_ref[t * rows : (t + 1) * rows, :] = standard_rows(
            across[t - 1][...], direct, people_all
        )
    std_ref[...] = standard_rows(single_ref[...], crossed, people_all)
    sent_ref[...] = scaled_product(std_ref[...], wide_ref[...])


def multiply_early(role, people_all, own, passed, single, direct, crossed, across):
    half = 1 + len(across)
    rows, markers = own.shape
    vmem = pl.BlockSpec(memory_space=pltpu.VMEM)
    return pl.pallas_call(
        functools.partial(early_kernel, half, people_all),
        out_shape=(
            jax.ShapeDtypeStruct((half * rows, markers), jnp.bfloat16),
            jax.ShapeDtypeStruct((rows, markers), jnp.bfloat16),
            jax.ShapeDtypeStruct((rows, half * rows), jnp.bfloat16),
        ),
        in_specs=[pl.BlockSpec(memory_space=pltpu.SMEM)] + [vmem] * (5 + len(across)),
        out_specs=[vmem] * 3,
        cost_estimate=pl.CostEstimate(
            flops=2 * rows * half * rows * markers,
            bytes_accessed=2 * (half + 2) * rows * markers,
            transcendentals=0,
        ),
        compiler_params=pltpu.CompilerParams(vmem_limit_bytes=VMEM_BYTES),
    )(role, own, passed, single, direct, crossed, *across)


def late_kernel(half, people_all, *refs):
    wide_ref, std_ref, crossed_ref = refs[:3]
    singles, sent_refs = refs[3 : half + 2], refs[half + 2 : 2 * half + 1]
    kept_refs, all_ref = refs[2 * half + 1 : -1], refs[-1]
    rows = std_ref.shape[0]
    all_ref[:rows, :] = std_ref[...]
    for t in range(1, half):
        all_ref[t * rows : (t + 1) * rows, :] = standard_rows(
            singles[t - 1][...], crossed_ref[...], people_all
        )
    sent = scaled_product(all_ref[rows:, :], wide_ref[...])
    for t in range(1, half):
        sent_refs[t - 1][...] = sent[(t - 1) * rows : t * rows]
    kept = scaled_product(wide_ref[...], all_ref[...])
    for t in range(half):
        kept_refs[t][...] = kept[t * rows : (t + 1) * rows]


def multiply_late(people_all, wide, std, crossed, singles):
    half = 1 + len(singles)
    rows, markers = std.shape
    vmem = pl.BlockSpec(memory_space=pltpu.VMEM)
    outs = pl.pallas_call(
        functools.partial(late_kernel, half, people_all),
        out_shape=[jax.ShapeDtypeStruct((rows, half * rows), jnp.bfloat16)] * (2 * half - 1),
        in_specs=[vmem] * (2 + half),
        out_specs=[vmem] * (2 * half - 1),
        scratch_shapes=[pltpu.VMEM((half * rows, markers), jnp.bfloat16)],
        cost_estimate=pl.CostEstimate(
            flops=4 * half * half * rows * rows * markers,
            bytes_accessed=4 * half * rows * markers,
            transcendentals=0,
        ),
        compiler_params=pltpu.CompilerParams(vmem_limit_bytes=VMEM_BYTES),
    )(wide, std, crossed, *singles)
    return list(outs[: half - 1]), list(outs[half - 1 :])


def place_kernel(half, role_ref, *refs):
    sent, kept, out_ref = refs[:half], refs[half:-1], refs[-1]
    rows = out_ref.shape[1]
    place = role_ref[1]
    near = 2 * half

    def put(block, part, column):
        to = pl.ds(pl.multiple_of(block * rows, rows), rows)
        out_ref[0, :, to] = part[:, column * rows : (column + 1) * rows]

    @pl.when(role_ref[0] == 1)
    def _():
        for t in range(half):
            for part, chip in ((kept[t], place ^ 2 * t), (sent[t], place ^ 2 * t + 1)):
                for m in range(half):
                    put(chip ^ near * m, part, m)

    @pl.when(role_ref[0] == 0)
    def _():
        for t in range(half):
            chip = place ^ near * t
            for d in range(half):
                put(chip ^ 2 * d, sent[t], d)
                put(chip ^ 2 * d + 1, kept[t], d)


def place_blocks(role, half, sent, kept):
    rows = sent[0].shape[0]
    vmem = pl.BlockSpec(memory_space=pltpu.VMEM)
    return pl.pallas_call(
        functools.partial(place_kernel, half),
        out_shape=jax.ShapeDtypeStruct((1, rows, 2 * half * half * rows), jnp.bfloat16),
        in_specs=[pl.BlockSpec(memory_space=pltpu.SMEM)] + [vmem] * (2 * half),
        out_specs=vmem,
        compiler_params=pltpu.CompilerParams(vmem_limit_bytes=VMEM_BYTES),
    )(role, *sent, *kept)


def one_round(round_number, cohorts, blocks, own, spread):
    half = half_size(blocks)
    near = 2 * half
    left = left_cohorts(cohorts, round_number)

    def send(value, *legs):
        pairs = []
        for c in left:
            for i in range(blocks):
                for leg in legs:
                    (c0, i0), (c1, i1) = leg(c, i)
                    pairs.append((c0 * blocks + i0, c1 * blocks + i1))
        return lax.ppermute(value, AXES, pairs)

    def left_to_left(d):
        return lambda c, i: ((c, i), (c, i ^ d))

    def left_to_mate(d):
        return lambda c, i: ((c, i), (c ^ 1, i ^ d))

    def mate_to_left(d):
        return lambda c, i: ((c ^ 1, i), (c, i ^ d))

    def mate_to_mate(d):
        return lambda c, i: ((c ^ 1, i), (c ^ 1, i ^ d))

    def owner_to_left(c, i):
        return (c ^ round_number, i), (c, i)

    def owner_to_mate(c, i):
        return (c ^ round_number, i), (c ^ 1, i)

    def right_rows_to_mate(t):
        return lambda c, i: ((c ^ 1, i), (c ^ round_number, i ^ near * t))

    def right_rows_to_left(c, i):
        return (c, i), (c ^ 1 ^ round_number, i)

    def left_to_owner(t):
        return lambda c, i: ((c, i), (c ^ round_number, i ^ near * t))

    def mate_to_owner(t):
        return lambda c, i: ((c ^ 1, i), (c ^ round_number, i ^ near * t))

    cohort = lax.axis_index("cohort")
    is_left = functools.reduce(jnp.logical_or, [cohort == c for c in left])
    role = jnp.stack([is_left.astype(jnp.int32), lax.axis_index("person")])

    first = [own] + [
        send(own, left_to_left(2 * t), right_rows_to_mate(t)) for t in range(1, half)
    ]
    beside = send(own, left_to_mate(0), mate_to_left(0))
    second = [send(beside, right_rows_to_left, mate_to_mate(1))]
    spread, _ = lax.optimization_barrier((spread, beside))
    totals = sum_of(lax.all_to_all(spread, "person", 0, 0, tiled=True))
    *first[1:], second[0], totals = lax.optimization_barrier((*first[1:], second[0], totals))
    second += [send(first[t], left_to_mate(1), mate_to_left(0)) for t in range(1, half)]
    passed = send(second[0], left_to_mate(0), mate_to_left(0))
    crossed = send(totals, left_to_mate(0), owner_to_left)
    direct = totals
    if round_number != 1:
        direct = send(totals, left_to_left(0), owner_to_mate)
    people_all = own.shape[0] * blocks
    wide, std, sent = multiply_early(
        role, people_all, own, passed, second[0], direct, crossed, first[1:]
    )
    early = send(sent, mate_to_left(1), left_to_owner(0))
    *second[1:], early = lax.optimization_barrier((*second[1:], early))
    sent, kept = multiply_late(people_all, wide, std, crossed, second[1:])
    sent = [early] + [
        send(sent[t - 1], mate_to_left(2 * t + 1), left_to_owner(t)) for t in range(1, half)
    ]
    for t in reversed(range(half)):
        if t or round_number != 1:
            kept[t] = send(kept[t], left_to_left(2 * t), mate_to_owner(t))
    return place_blocks(role, half, sent, kept)


def on_device(dosages, allele_counts, partner):
    cohorts, blocks = lax.axis_size("cohort"), lax.axis_size("person")
    rounds = [
        functools.partial(one_round, round_number, cohorts, blocks)
        for round_number in range(1, cohorts)
    ]
    index, spread, own = load(partner, allele_counts[0], dosages[0], blocks)
    return lax.switch(index[0], rounds, own, spread)


def solution(mesh):
    placed = (P("cohort", "person", None), P("cohort", "person", None), P())
    return jax.shard_map(
        on_device,
        mesh=mesh,
        in_specs=placed,
        out_specs=P("cohort", "person", None),
        check_vma=False,
    )
```

```python
import functools
import math

import jax
import jax.numpy as jnp
from jax import lax
from jax.experimental import pallas as pl
from jax.experimental.pallas import tpu as pltpu
from jax.sharding import PartitionSpec as P

AXES = ("cohort", "person")
VMEM_BYTES = 48 * 1024 * 1024
VMEM_WHOLE = 64 * 1024 * 1024
VMEM_ROOM = 128 * 1024


def left_cohorts(cohorts, round_number):
    if round_number == 1:
        return [c for c in range(cohorts) if c & 1 == 0]
    top = 1 << (round_number.bit_length() - 1)
    return [
        c
        for c in range(cohorts)
        if (c & top == 0 and c & 1 == 0) or (c & top and (c ^ round_number ^ 1) & 1 == 0)
    ]


def half_size(blocks):
    return 1 << (blocks.bit_length() // 2 - 1)


def load_kernel(rows_ref, counts_ref, rows_out, counts_out, sems):
    copies = [
        pltpu.make_async_copy(rows_ref, rows_out, sems.at[0]),
        pltpu.make_async_copy(counts_ref, counts_out, sems.at[1]),
    ]
    for copy in copies:
        copy.start()
    for copy in copies:
        copy.wait()


def load(rows, counts):
    arrays = (rows, counts)
    held = sum(array.size * array.dtype.itemsize for array in arrays)
    return pl.pallas_call(
        load_kernel,
        out_shape=[jax.ShapeDtypeStruct(array.shape, array.dtype) for array in arrays],
        in_specs=[pl.BlockSpec(memory_space=pl.ANY)] * 2,
        out_specs=[pl.BlockSpec(memory_space=pltpu.VMEM)] * 2,
        scratch_shapes=[pltpu.SemaphoreType.DMA((2,))],
        cost_estimate=pl.CostEstimate(flops=0, bytes_accessed=4 * held, transcendentals=0),
        compiler_params=pltpu.CompilerParams(vmem_limit_bytes=VMEM_WHOLE - VMEM_ROOM - held),
    )(*arrays)


def sum_kernel(parts_ref, out_ref):
    total = parts_ref[0]
    for n in range(1, parts_ref.shape[0]):
        total = total + parts_ref[n]
    out_ref[...] = total


def sum_of(parts):
    vmem = pl.BlockSpec(memory_space=pltpu.VMEM)
    return pl.pallas_call(
        sum_kernel,
        out_shape=jax.ShapeDtypeStruct(parts.shape[1:], parts.dtype),
        in_specs=[vmem],
        out_specs=vmem,
        compiler_params=pltpu.CompilerParams(vmem_limit_bytes=VMEM_BYTES),
    )(parts)


def standard_rows(rows, totals, people_all):
    freq = (totals.astype(jnp.float32) + 1.0) / (2.0 * people_all + 2.0)
    scale = 1.0 / jnp.sqrt(2.0 * freq * (1.0 - freq))
    return ((rows.astype(jnp.float32) - 2.0 * freq) * scale).astype(jnp.bfloat16)


def scaled_product(one, other):
    dims = (((1,), (1,)), ((), ()))
    out = lax.dot_general(one, other, dims, preferred_element_type=jnp.float32)
    return (out / math.sqrt(one.shape[1])).astype(jnp.bfloat16)


def early_kernel(half, people_all, role_ref, *refs):
    own_ref, passed_ref, single_ref, totals_ref = refs[:4]
    across, (wide_ref, std_ref, sent_ref) = refs[4:-3], refs[-3:]
    rows = own_ref.shape[0]
    direct, crossed = totals_ref[0], totals_ref[1]

    @pl.when(role_ref[0] == 1)
    def _():
        wide_ref[:rows, :] = standard_rows(own_ref[...], direct, people_all)

    @pl.when(role_ref[0] == 0)
    def _():
        wide_ref[:rows, :] = standard_rows(passed_ref[...], direct, people_all)

    for t in range(1, half):
        wide_ref[t * rows : (t + 1) * rows, :] = standard_rows(
            across[t - 1][...], direct, people_all
        )
    std_ref[...] = standard_rows(single_ref[...], crossed, people_all)
    sent_ref[...] = scaled_product(std_ref[...], wide_ref[...])


def multiply_early(role, people_all, own, passed, single, totals, across):
    half = 1 + len(across)
    rows, markers = own.shape
    vmem = pl.BlockSpec(memory_space=pltpu.VMEM)
    return pl.pallas_call(
        functools.partial(early_kernel, half, people_all),
        out_shape=(
            jax.ShapeDtypeStruct((half * rows, markers), jnp.bfloat16),
            jax.ShapeDtypeStruct((rows, markers), jnp.bfloat16),
            jax.ShapeDtypeStruct((rows, half * rows), jnp.bfloat16),
        ),
        in_specs=[pl.BlockSpec(memory_space=pltpu.SMEM)] + [vmem] * (4 + len(across)),
        out_specs=[vmem] * 3,
        cost_estimate=pl.CostEstimate(
            flops=2 * rows * half * rows * markers,
            bytes_accessed=2 * (half + 2) * rows * markers,
            transcendentals=0,
        ),
        compiler_params=pltpu.CompilerParams(vmem_limit_bytes=VMEM_BYTES),
    )(role, own, passed, single, totals, *across)


def late_kernel(half, people_all, *refs):
    wide_ref, std_ref, totals_ref = refs[:3]
    singles, sent_refs = refs[3 : half + 2], refs[half + 2 : 2 * half + 1]
    kept_refs, all_ref = refs[2 * half + 1 : -1], refs[-1]
    rows = std_ref.shape[0]
    all_ref[:rows, :] = std_ref[...]
    for t in range(1, half):
        all_ref[t * rows : (t + 1) * rows, :] = standard_rows(
            singles[t - 1][...], totals_ref[1], people_all
        )
    sent = scaled_product(all_ref[rows:, :], wide_ref[...])
    for t in range(1, half):
        sent_refs[t - 1][...] = sent[(t - 1) * rows : t * rows]
    kept = scaled_product(wide_ref[...], all_ref[...])
    for t in range(half):
        kept_refs[t][...] = kept[t * rows : (t + 1) * rows]


def multiply_late(people_all, wide, std, totals, singles):
    half = 1 + len(singles)
    rows, markers = std.shape
    vmem = pl.BlockSpec(memory_space=pltpu.VMEM)
    outs = pl.pallas_call(
        functools.partial(late_kernel, half, people_all),
        out_shape=[jax.ShapeDtypeStruct((rows, half * rows), jnp.bfloat16)] * (2 * half - 1),
        in_specs=[vmem] * (2 + half),
        out_specs=[vmem] * (2 * half - 1),
        scratch_shapes=[pltpu.VMEM((half * rows, markers), jnp.bfloat16)],
        cost_estimate=pl.CostEstimate(
            flops=4 * half * half * rows * rows * markers,
            bytes_accessed=4 * half * rows * markers,
            transcendentals=0,
        ),
        compiler_params=pltpu.CompilerParams(vmem_limit_bytes=VMEM_BYTES),
    )(wide, std, totals, *singles)
    return list(outs[: half - 1]), list(outs[half - 1 :])


def place_kernel(half, role_ref, *refs):
    sent, kept, out_ref = refs[:half], refs[half:-1], refs[-1]
    rows = out_ref.shape[1]
    place = role_ref[1]
    near = 2 * half

    def put(block, part, column):
        to = pl.ds(pl.multiple_of(block * rows, rows), rows)
        out_ref[0, :, to] = part[:, column * rows : (column + 1) * rows]

    @pl.when(role_ref[0] == 1)
    def _():
        for t in range(half):
            for part, chip in ((kept[t], place ^ 2 * t), (sent[t], place ^ 2 * t + 1)):
                for m in range(half):
                    put(chip ^ near * m, part, m)

    @pl.when(role_ref[0] == 0)
    def _():
        for t in range(half):
            chip = place ^ near * t
            for d in range(half):
                put(chip ^ 2 * d, sent[t], d)
                put(chip ^ 2 * d + 1, kept[t], d)


def place_blocks(role, half, sent, kept):
    rows = sent[0].shape[0]
    vmem = pl.BlockSpec(memory_space=pltpu.VMEM)
    return pl.pallas_call(
        functools.partial(place_kernel, half),
        out_shape=jax.ShapeDtypeStruct((1, rows, 2 * half * half * rows), jnp.bfloat16),
        in_specs=[pl.BlockSpec(memory_space=pltpu.SMEM)] + [vmem] * (2 * half),
        out_specs=vmem,
        compiler_params=pltpu.CompilerParams(vmem_limit_bytes=VMEM_BYTES),
    )(role, *sent, *kept)


def one_round(round_number, cohorts, blocks, own, counts):
    half = half_size(blocks)
    near = 2 * half
    left = left_cohorts(cohorts, round_number)

    def send(value, *legs):
        pairs = []
        for c in left:
            for i in range(blocks):
                for leg in legs:
                    (c0, i0), (c1, i1) = leg(c, i)
                    pairs.append((c0 * blocks + i0, c1 * blocks + i1))
        return lax.ppermute(value, AXES, pairs)

    def left_to_left(d):
        return lambda c, i: ((c, i), (c, i ^ d))

    def left_to_mate(d):
        return lambda c, i: ((c, i), (c ^ 1, i ^ d))

    def mate_to_left(d):
        return lambda c, i: ((c ^ 1, i), (c, i ^ d))

    def owner_to_left(c, i):
        return (c ^ round_number, i), (c, i)

    def owner_to_mate(c, i):
        return (c ^ round_number, i), (c ^ 1, i)

    def right_rows_to_mate(t):
        return lambda c, i: ((c ^ 1, i), (c ^ round_number, i ^ near * t))

    def left_to_owner(t):
        return lambda c, i: ((c, i), (c ^ round_number, i ^ near * t))

    def mate_to_owner(t):
        return lambda c, i: ((c ^ 1, i), (c ^ round_number, i ^ near * t))

    cohort = lax.axis_index("cohort")
    is_left = functools.reduce(jnp.logical_or, [cohort == c for c in left])
    role = jnp.stack([is_left.astype(jnp.int32), lax.axis_index("person")])

    first = [own] + [
        send(own, left_to_left(2 * t), right_rows_to_mate(t)) for t in range(1, half)
    ]
    second = [send(own, left_to_mate(1), owner_to_left)]
    crossed = send(counts, left_to_mate(0), owner_to_left)
    direct = counts
    if round_number != 1:
        direct = send(counts, left_to_left(0), owner_to_mate)
    both = jnp.stack([direct, crossed])
    spread = jnp.broadcast_to(both[None], (blocks, *both.shape))
    totals = sum_of(lax.all_to_all(spread, "person", 0, 0, tiled=True))
    *first[1:], second[0], totals = lax.optimization_barrier((*first[1:], second[0], totals))
    second += [send(first[t], left_to_mate(1), mate_to_left(0)) for t in range(1, half)]
    passed = send(second[0], left_to_mate(0), mate_to_left(0))
    people_all = own.shape[0] * blocks
    wide, std, sent = multiply_early(
        role, people_all, own, passed, second[0], totals, first[1:]
    )
    late, kept = multiply_late(people_all, wide, std, totals, second[1:])
    sent = list(lax.optimization_barrier((sent, *late)))
    for t in reversed(range(half)):
        sent[t] = send(sent[t], mate_to_left(2 * t + 1), left_to_owner(t))
        if t or round_number != 1:
            kept[t] = send(kept[t], left_to_left(2 * t), mate_to_owner(t))
    return place_blocks(role, half, sent, kept)


def on_device(dosages, allele_counts, partner):
    cohorts, blocks = lax.axis_size("cohort"), lax.axis_size("person")
    rounds = [
        functools.partial(one_round, round_number, cohorts, blocks)
        for round_number in range(1, cohorts)
    ]
    return lax.switch(partner[0] - 1, rounds, *load(dosages[0], allele_counts[0]))


def solution(mesh):
    placed = (P("cohort", "person", None), P("cohort", "person", None), P())
    return jax.shard_map(
        on_device,
        mesh=mesh,
        in_specs=placed,
        out_specs=P("cohort", "person", None),
        check_vma=False,
    )
```

```python
import functools
import math

import jax
import jax.numpy as jnp
from jax import lax
from jax.experimental import pallas as pl
from jax.experimental.pallas import tpu as pltpu
from jax.sharding import PartitionSpec as P

AXES = ("cohort", "person")
VMEM_BYTES = 48 * 1024 * 1024
VMEM_WHOLE = 64 * 1024 * 1024
VMEM_ROOM = 128 * 1024


def left_cohorts(cohorts, round_number):
    if round_number == 1:
        return [c for c in range(cohorts) if c & 1 == 0]
    top = 1 << (round_number.bit_length() - 1)
    return [
        c
        for c in range(cohorts)
        if (c & top == 0 and c & 1 == 0) or (c & top and (c ^ round_number ^ 1) & 1 == 0)
    ]


def half_size(blocks):
    return 1 << (blocks.bit_length() // 2 - 1)


def load_kernel(rows_ref, counts_ref, rows_out, counts_out, sems):
    copies = [
        pltpu.make_async_copy(rows_ref, rows_out, sems.at[0]),
        pltpu.make_async_copy(counts_ref, counts_out, sems.at[1]),
    ]
    for copy in copies:
        copy.start()
    for copy in copies:
        copy.wait()


def load(rows, counts):
    arrays = (rows, counts)
    held = sum(array.size * array.dtype.itemsize for array in arrays)
    return pl.pallas_call(
        load_kernel,
        out_shape=[jax.ShapeDtypeStruct(array.shape, array.dtype) for array in arrays],
        in_specs=[pl.BlockSpec(memory_space=pl.ANY)] * 2,
        out_specs=[pl.BlockSpec(memory_space=pltpu.VMEM)] * 2,
        scratch_shapes=[pltpu.SemaphoreType.DMA((2,))],
        cost_estimate=pl.CostEstimate(flops=0, bytes_accessed=4 * held, transcendentals=0),
        compiler_params=pltpu.CompilerParams(vmem_limit_bytes=VMEM_WHOLE - VMEM_ROOM - held),
    )(*arrays)


def sum_kernel(parts_ref, out_ref):
    total = parts_ref[0]
    for n in range(1, parts_ref.shape[0]):
        total = total + parts_ref[n]
    out_ref[...] = total


def sum_of(parts):
    vmem = pl.BlockSpec(memory_space=pltpu.VMEM)
    return pl.pallas_call(
        sum_kernel,
        out_shape=jax.ShapeDtypeStruct(parts.shape[1:], parts.dtype),
        in_specs=[vmem],
        out_specs=vmem,
        compiler_params=pltpu.CompilerParams(vmem_limit_bytes=VMEM_BYTES),
    )(parts)


def standard_rows(rows, totals, people_all):
    freq = (totals.astype(jnp.float32) + 1.0) / (2.0 * people_all + 2.0)
    scale = 1.0 / jnp.sqrt(2.0 * freq * (1.0 - freq))
    return ((rows.astype(jnp.float32) - 2.0 * freq) * scale).astype(jnp.bfloat16)


def scaled_product(one, other):
    dims = (((1,), (1,)), ((), ()))
    out = lax.dot_general(one, other, dims, preferred_element_type=jnp.float32)
    return (out / math.sqrt(one.shape[1])).astype(jnp.bfloat16)


def early_kernel(half, people_all, role_ref, *refs):
    own_ref, passed_ref, single_ref, direct_ref, crossed_ref = refs[:5]
    across, (wide_ref, std_ref, sent_ref) = refs[5:-3], refs[-3:]
    rows = own_ref.shape[0]
    direct, crossed = direct_ref[...], crossed_ref[...]

    @pl.when(role_ref[0] == 1)
    def _():
        wide_ref[:rows, :] = standard_rows(own_ref[...], direct, people_all)

    @pl.when(role_ref[0] == 0)
    def _():
        wide_ref[:rows, :] = standard_rows(passed_ref[...], direct, people_all)

    for t in range(1, half):
        wide_ref[t * rows : (t + 1) * rows, :] = standard_rows(
            across[t - 1][...], direct, people_all
        )
    std_ref[...] = standard_rows(single_ref[...], crossed, people_all)
    sent_ref[...] = scaled_product(std_ref[...], wide_ref[...])


def multiply_early(role, people_all, own, passed, single, direct, crossed, across):
    half = 1 + len(across)
    rows, markers = own.shape
    vmem = pl.BlockSpec(memory_space=pltpu.VMEM)
    return pl.pallas_call(
        functools.partial(early_kernel, half, people_all),
        out_shape=(
            jax.ShapeDtypeStruct((half * rows, markers), jnp.bfloat16),
            jax.ShapeDtypeStruct((rows, markers), jnp.bfloat16),
            jax.ShapeDtypeStruct((rows, half * rows), jnp.bfloat16),
        ),
        in_specs=[pl.BlockSpec(memory_space=pltpu.SMEM)] + [vmem] * (5 + len(across)),
        out_specs=[vmem] * 3,
        cost_estimate=pl.CostEstimate(
            flops=2 * rows * half * rows * markers,
            bytes_accessed=2 * (half + 2) * rows * markers,
            transcendentals=0,
        ),
        compiler_params=pltpu.CompilerParams(vmem_limit_bytes=VMEM_BYTES),
    )(role, own, passed, single, direct, crossed, *across)


def late_kernel(half, people_all, *refs):
    wide_ref, std_ref, crossed_ref = refs[:3]
    singles, sent_refs = refs[3 : half + 2], refs[half + 2 : 2 * half + 1]
    kept_refs, all_ref = refs[2 * half + 1 : -1], refs[-1]
    rows = std_ref.shape[0]
    all_ref[:rows, :] = std_ref[...]
    for t in range(1, half):
        all_ref[t * rows : (t + 1) * rows, :] = standard_rows(
            singles[t - 1][...], crossed_ref[...], people_all
        )
    sent = scaled_product(all_ref[rows:, :], wide_ref[...])
    for t in range(1, half):
        sent_refs[t - 1][...] = sent[(t - 1) * rows : t * rows]
    kept = scaled_product(wide_ref[...], all_ref[...])
    for t in range(half):
        kept_refs[t][...] = kept[t * rows : (t + 1) * rows]


def multiply_late(people_all, wide, std, crossed, singles):
    half = 1 + len(singles)
    rows, markers = std.shape
    vmem = pl.BlockSpec(memory_space=pltpu.VMEM)
    outs = pl.pallas_call(
        functools.partial(late_kernel, half, people_all),
        out_shape=[jax.ShapeDtypeStruct((rows, half * rows), jnp.bfloat16)] * (2 * half - 1),
        in_specs=[vmem] * (2 + half),
        out_specs=[vmem] * (2 * half - 1),
        scratch_shapes=[pltpu.VMEM((half * rows, markers), jnp.bfloat16)],
        cost_estimate=pl.CostEstimate(
            flops=4 * half * half * rows * rows * markers,
            bytes_accessed=4 * half * rows * markers,
            transcendentals=0,
        ),
        compiler_params=pltpu.CompilerParams(vmem_limit_bytes=VMEM_BYTES),
    )(wide, std, crossed, *singles)
    return list(outs[: half - 1]), list(outs[half - 1 :])


def place_kernel(half, role_ref, *refs):
    sent, kept, out_ref = refs[:half], refs[half:-1], refs[-1]
    rows = out_ref.shape[1]
    place = role_ref[1]
    near = 2 * half

    def put(block, part, column):
        to = pl.ds(pl.multiple_of(block * rows, rows), rows)
        out_ref[0, :, to] = part[:, column * rows : (column + 1) * rows]

    @pl.when(role_ref[0] == 1)
    def _():
        for t in range(half):
            for part, chip in ((kept[t], place ^ 2 * t), (sent[t], place ^ 2 * t + 1)):
                for m in range(half):
                    put(chip ^ near * m, part, m)

    @pl.when(role_ref[0] == 0)
    def _():
        for t in range(half):
            chip = place ^ near * t
            for d in range(half):
                put(chip ^ 2 * d, sent[t], d)
                put(chip ^ 2 * d + 1, kept[t], d)


def place_blocks(role, half, sent, kept):
    rows = sent[0].shape[0]
    vmem = pl.BlockSpec(memory_space=pltpu.VMEM)
    return pl.pallas_call(
        functools.partial(place_kernel, half),
        out_shape=jax.ShapeDtypeStruct((1, rows, 2 * half * half * rows), jnp.bfloat16),
        in_specs=[pl.BlockSpec(memory_space=pltpu.SMEM)] + [vmem] * (2 * half),
        out_specs=vmem,
        compiler_params=pltpu.CompilerParams(vmem_limit_bytes=VMEM_BYTES),
    )(role, *sent, *kept)


def one_round(round_number, cohorts, blocks, own, counts):
    half = half_size(blocks)
    near = 2 * half
    left = left_cohorts(cohorts, round_number)

    def send(value, *legs):
        pairs = []
        for c in left:
            for i in range(blocks):
                for leg in legs:
                    (c0, i0), (c1, i1) = leg(c, i)
                    pairs.append((c0 * blocks + i0, c1 * blocks + i1))
        return lax.ppermute(value, AXES, pairs)

    def left_to_left(d):
        return lambda c, i: ((c, i), (c, i ^ d))

    def left_to_mate(d):
        return lambda c, i: ((c, i), (c ^ 1, i ^ d))

    def mate_to_left(d):
        return lambda c, i: ((c ^ 1, i), (c, i ^ d))

    def mate_to_mate(d):
        return lambda c, i: ((c ^ 1, i), (c ^ 1, i ^ d))

    def owner_to_left(c, i):
        return (c ^ round_number, i), (c, i)

    def owner_to_mate(c, i):
        return (c ^ round_number, i), (c ^ 1, i)

    def right_rows_to_mate(t):
        return lambda c, i: ((c ^ 1, i), (c ^ round_number, i ^ near * t))

    def right_rows_to_left(c, i):
        return (c, i), (c ^ 1 ^ round_number, i)

    def left_to_owner(t):
        return lambda c, i: ((c, i), (c ^ round_number, i ^ near * t))

    def mate_to_owner(t):
        return lambda c, i: ((c ^ 1, i), (c ^ round_number, i ^ near * t))

    cohort = lax.axis_index("cohort")
    is_left = functools.reduce(jnp.logical_or, [cohort == c for c in left])
    role = jnp.stack([is_left.astype(jnp.int32), lax.axis_index("person")])

    first = [own] + [
        send(own, left_to_left(2 * t), right_rows_to_mate(t)) for t in range(1, half)
    ]
    beside = send(own, left_to_mate(0), mate_to_left(0))
    second = [send(beside, right_rows_to_left, mate_to_mate(1))]
    counts, _ = lax.optimization_barrier((counts, beside))
    spread = jnp.broadcast_to(counts[None], (blocks, *counts.shape))
    totals = sum_of(lax.all_to_all(spread, "person", 0, 0, tiled=True))
    *first[1:], totals = lax.optimization_barrier((*first[1:], totals))
    second[0], _ = lax.optimization_barrier((second[0], first[1]))
    second += [send(first[t], left_to_mate(1), mate_to_left(0)) for t in range(1, half)]
    passed = send(second[0], left_to_mate(0), mate_to_left(0))
    crossed = send(totals, left_to_mate(0), owner_to_left)
    direct = totals
    if round_number != 1:
        direct = send(totals, left_to_left(0), owner_to_mate)
    people_all = own.shape[0] * blocks
    wide, std, sent = multiply_early(
        role, people_all, own, passed, second[0], direct, crossed, first[1:]
    )
    late, kept = multiply_late(people_all, wide, std, crossed, second[1:])
    sent = list(lax.optimization_barrier((sent, *late)))
    for t in reversed(range(half)):
        sent[t] = send(sent[t], mate_to_left(2 * t + 1), left_to_owner(t))
        if t or round_number != 1:
            kept[t] = send(kept[t], left_to_left(2 * t), mate_to_owner(t))
    return place_blocks(role, half, sent, kept)


def on_device(dosages, allele_counts, partner):
    cohorts, blocks = lax.axis_size("cohort"), lax.axis_size("person")
    rounds = [
        functools.partial(one_round, round_number, cohorts, blocks)
        for round_number in range(1, cohorts)
    ]
    return lax.switch(partner[0] - 1, rounds, *load(dosages[0], allele_counts[0]))


def solution(mesh):
    placed = (P("cohort", "person", None), P("cohort", "person", None), P())
    return jax.shard_map(
        on_device,
        mesh=mesh,
        in_specs=placed,
        out_specs=P("cohort", "person", None),
        check_vma=False,
    )
```

```python
import functools
import math

import jax
import jax.numpy as jnp
from jax import lax
from jax.experimental import pallas as pl
from jax.experimental.pallas import tpu as pltpu
from jax.sharding import PartitionSpec as P

AXES = ("cohort", "person")
VMEM_BYTES = 48 * 1024 * 1024
VMEM_WHOLE = 64 * 1024 * 1024
VMEM_ROOM = 128 * 1024


def left_cohorts(cohorts, round_number):
    if round_number == 1:
        return [c for c in range(cohorts) if c & 1 == 0]
    top = 1 << (round_number.bit_length() - 1)
    return [
        c
        for c in range(cohorts)
        if (c & top == 0 and c & 1 == 0) or (c & top and (c ^ round_number ^ 1) & 1 == 0)
    ]


def half_size(blocks):
    return 1 << (blocks.bit_length() // 2 - 1)


def load_kernel(rows_ref, counts_ref, rows_out, counts_out, sems):
    copies = [
        pltpu.make_async_copy(rows_ref, rows_out, sems.at[0]),
        pltpu.make_async_copy(counts_ref, counts_out, sems.at[1]),
    ]
    for copy in copies:
        copy.start()
    for copy in copies:
        copy.wait()


def load(rows, counts):
    arrays = (rows, counts)
    held = sum(array.size * array.dtype.itemsize for array in arrays)
    return pl.pallas_call(
        load_kernel,
        out_shape=[jax.ShapeDtypeStruct(array.shape, array.dtype) for array in arrays],
        in_specs=[pl.BlockSpec(memory_space=pl.ANY)] * 2,
        out_specs=[pl.BlockSpec(memory_space=pltpu.VMEM)] * 2,
        scratch_shapes=[pltpu.SemaphoreType.DMA((2,))],
        cost_estimate=pl.CostEstimate(flops=0, bytes_accessed=4 * held, transcendentals=0),
        compiler_params=pltpu.CompilerParams(vmem_limit_bytes=VMEM_WHOLE - VMEM_ROOM - held),
    )(*arrays)


def sum_kernel(parts_ref, out_ref):
    total = parts_ref[0]
    for n in range(1, parts_ref.shape[0]):
        total = total + parts_ref[n]
    out_ref[...] = total


def sum_of(parts):
    vmem = pl.BlockSpec(memory_space=pltpu.VMEM)
    return pl.pallas_call(
        sum_kernel,
        out_shape=jax.ShapeDtypeStruct(parts.shape[1:], parts.dtype),
        in_specs=[vmem],
        out_specs=vmem,
        compiler_params=pltpu.CompilerParams(vmem_limit_bytes=VMEM_BYTES),
    )(parts)


def standard_rows(rows, totals, people_all):
    freq = (totals.astype(jnp.float32) + 1.0) / (2.0 * people_all + 2.0)
    scale = 1.0 / jnp.sqrt(2.0 * freq * (1.0 - freq))
    return ((rows.astype(jnp.float32) - 2.0 * freq) * scale).astype(jnp.bfloat16)


def scaled_product(one, other):
    dims = (((1,), (1,)), ((), ()))
    out = lax.dot_general(one, other, dims, preferred_element_type=jnp.float32)
    return (out / math.sqrt(one.shape[1])).astype(jnp.bfloat16)


def early_kernel(count, people_all, *refs):
    (direct_ref, crossed_ref), rows, outs = refs[:2], refs[2 : count + 2], refs[count + 2 :]
    for n in range(count):
        totals_ref = crossed_ref if n == count - 1 else direct_ref
        outs[n][...] = standard_rows(rows[n][...], totals_ref[...], people_all)


def standardize(people_all, direct, crossed, wide, single):
    rows = [*wide, single]
    vmem = pl.BlockSpec(memory_space=pltpu.VMEM)
    return pl.pallas_call(
        functools.partial(early_kernel, len(rows), people_all),
        out_shape=[jax.ShapeDtypeStruct(single.shape, single.dtype)] * len(rows),
        in_specs=[vmem] * (2 + len(rows)),
        out_specs=[vmem] * len(rows),
        compiler_params=pltpu.CompilerParams(vmem_limit_bytes=VMEM_BYTES),
    )(direct, crossed, *rows)


def late_kernel(half, people_all, role_ref, *refs):
    direct_ref, crossed_ref, passed_ref = refs[:3]
    standard, relayed = refs[3 : half + 4], refs[half + 4 : 2 * half + 3]
    outs, (wide_ref, all_ref) = refs[2 * half + 3 : -2], refs[-2:]
    sent_refs, kept_refs = outs[:half], outs[half:]
    rows = passed_ref.shape[0]

    @pl.when(role_ref[0] == 1)
    def _():
        wide_ref[:rows, :] = standard[0][...]

    @pl.when(role_ref[0] == 0)
    def _():
        wide_ref[:rows, :] = standard_rows(passed_ref[...], direct_ref[...], people_all)

    all_ref[:rows, :] = standard[half][...]
    for t in range(1, half):
        at = slice(t * rows, (t + 1) * rows)
        wide_ref[at, :] = standard[t][...]
        all_ref[at, :] = standard_rows(relayed[t - 1][...], crossed_ref[...], people_all)
    for one, other, outs in ((all_ref, wide_ref, sent_refs), (wide_ref, all_ref, kept_refs)):
        blocks = scaled_product(one[...], other[...])
        for t in range(half):
            outs[t][...] = blocks[t * rows : (t + 1) * rows]


def multiply(role, people_all, direct, crossed, passed, standard, relayed):
    half = len(standard) - 1
    rows, markers = passed.shape
    vmem = pl.BlockSpec(memory_space=pltpu.VMEM)
    outs = pl.pallas_call(
        functools.partial(late_kernel, half, people_all),
        out_shape=[jax.ShapeDtypeStruct((rows, half * rows), jnp.bfloat16)] * (2 * half),
        in_specs=[pl.BlockSpec(memory_space=pltpu.SMEM)] + [vmem] * (3 + 2 * half),
        out_specs=[vmem] * (2 * half),
        scratch_shapes=[pltpu.VMEM((half * rows, markers), jnp.bfloat16)] * 2,
        compiler_params=pltpu.CompilerParams(vmem_limit_bytes=VMEM_BYTES),
    )(role, direct, crossed, passed, *standard, *relayed)
    return list(outs[:half]), list(outs[half:])


def place_kernel(half, role_ref, *refs):
    sent, kept, out_ref = refs[:half], refs[half:-1], refs[-1]
    rows = out_ref.shape[1]
    place = role_ref[1]
    near = 2 * half

    def put(block, part, column):
        to = pl.ds(pl.multiple_of(block * rows, rows), rows)
        out_ref[0, :, to] = part[:, column * rows : (column + 1) * rows]

    @pl.when(role_ref[0] == 1)
    def _():
        for t in range(half):
            for part, chip in ((kept[t], place ^ 2 * t), (sent[t], place ^ 2 * t + 1)):
                for m in range(half):
                    put(chip ^ near * m, part, m)

    @pl.when(role_ref[0] == 0)
    def _():
        for t in range(half):
            chip = place ^ near * t
            for d in range(half):
                put(chip ^ 2 * d, sent[t], d)
                put(chip ^ 2 * d + 1, kept[t], d)


def place_blocks(role, half, sent, kept):
    rows = sent[0].shape[0]
    vmem = pl.BlockSpec(memory_space=pltpu.VMEM)
    return pl.pallas_call(
        functools.partial(place_kernel, half),
        out_shape=jax.ShapeDtypeStruct((1, rows, 2 * half * half * rows), jnp.bfloat16),
        in_specs=[pl.BlockSpec(memory_space=pltpu.SMEM)] + [vmem] * (2 * half),
        out_specs=vmem,
        compiler_params=pltpu.CompilerParams(vmem_limit_bytes=VMEM_BYTES),
    )(role, *sent, *kept)


def one_round(round_number, cohorts, blocks, own, counts):
    half = half_size(blocks)
    near = 2 * half
    left = left_cohorts(cohorts, round_number)

    def send(value, *legs):
        pairs = []
        for c in left:
            for i in range(blocks):
                for leg in legs:
                    (c0, i0), (c1, i1) = leg(c, i)
                    pairs.append((c0 * blocks + i0, c1 * blocks + i1))
        return lax.ppermute(value, AXES, pairs)

    def left_to_left(d):
        return lambda c, i: ((c, i), (c, i ^ d))

    def left_to_mate(d):
        return lambda c, i: ((c, i), (c ^ 1, i ^ d))

    def mate_to_left(d):
        return lambda c, i: ((c ^ 1, i), (c, i ^ d))

    def mate_to_mate(d):
        return lambda c, i: ((c ^ 1, i), (c ^ 1, i ^ d))

    def owner_to_left(c, i):
        return (c ^ round_number, i), (c, i)

    def owner_to_mate(c, i):
        return (c ^ round_number, i), (c ^ 1, i)

    def right_rows_to_mate(t):
        return lambda c, i: ((c ^ 1, i), (c ^ round_number, i ^ near * t))

    def right_rows_to_left(c, i):
        return (c, i), (c ^ 1 ^ round_number, i)

    def left_to_owner(t):
        return lambda c, i: ((c, i), (c ^ round_number, i ^ near * t))

    def mate_to_owner(t):
        return lambda c, i: ((c ^ 1, i), (c ^ round_number, i ^ near * t))

    cohort = lax.axis_index("cohort")
    is_left = functools.reduce(jnp.logical_or, [cohort == c for c in left])
    role = jnp.stack([is_left.astype(jnp.int32), lax.axis_index("person")])

    first = [own] + [
        send(own, left_to_left(2 * t), right_rows_to_mate(t)) for t in range(1, half)
    ]
    beside = send(own, left_to_mate(0), mate_to_left(0))
    second = [send(beside, right_rows_to_left, mate_to_mate(1))]
    counts, _ = lax.optimization_barrier((counts, beside))
    spread = jnp.broadcast_to(counts[None], (blocks, *counts.shape))
    totals = sum_of(lax.all_to_all(spread, "person", 0, 0, tiled=True))
    *first[1:], totals = lax.optimization_barrier((*first[1:], totals))
    second += [send(first[t], left_to_mate(1), mate_to_left(0)) for t in range(1, half)]
    passed = send(second[0], left_to_mate(0), mate_to_left(0))
    crossed = send(totals, left_to_mate(0), owner_to_left)
    direct = totals
    if round_number != 1:
        direct = send(totals, left_to_left(0), owner_to_mate)
    people_all = own.shape[0] * blocks
    standard = standardize(people_all, direct, crossed, first, second[0])
    sent, kept = multiply(role, people_all, direct, crossed, passed, standard, second[1:])
    for t in reversed(range(1, half)):
        sent[t] = send(sent[t], mate_to_left(2 * t + 1), left_to_owner(t))
        kept[t] = send(kept[t], left_to_left(2 * t), mate_to_owner(t))
    if round_number != 1:
        kept[0] = send(kept[0], left_to_left(0), mate_to_owner(0))
    sent[0] = send(sent[0], mate_to_left(1), left_to_owner(0))
    return place_blocks(role, half, sent, kept)


def on_device(dosages, allele_counts, partner):
    cohorts, blocks = lax.axis_size("cohort"), lax.axis_size("person")
    rounds = [
        functools.partial(one_round, round_number, cohorts, blocks)
        for round_number in range(1, cohorts)
    ]
    return lax.switch(partner[0] - 1, rounds, *load(dosages[0], allele_counts[0]))


def solution(mesh):
    placed = (P("cohort", "person", None), P("cohort", "person", None), P())
    return jax.shard_map(
        on_device,
        mesh=mesh,
        in_specs=placed,
        out_specs=P("cohort", "person", None),
        check_vma=False,
    )
```

```python
import functools
import math

import jax
import jax.numpy as jnp
from jax import lax
from jax.experimental import pallas as pl
from jax.experimental.pallas import tpu as pltpu
from jax.sharding import PartitionSpec as P

AXES = ("cohort", "person")
VMEM_BYTES = 48 * 1024 * 1024
VMEM_WHOLE = 64 * 1024 * 1024
VMEM_ROOM = 128 * 1024


def left_cohorts(cohorts, round_number):
    if round_number == 1:
        return [c for c in range(cohorts) if c & 1 == 0]
    top = 1 << (round_number.bit_length() - 1)
    return [
        c
        for c in range(cohorts)
        if (c & top == 0 and c & 1 == 0) or (c & top and (c ^ round_number ^ 1) & 1 == 0)
    ]


def half_size(blocks):
    return 1 << (blocks.bit_length() // 2 - 1)


def load_kernel(rows_ref, counts_ref, rows_out, counts_out, sems):
    copies = [
        pltpu.make_async_copy(rows_ref, rows_out, sems.at[0]),
        pltpu.make_async_copy(counts_ref, counts_out, sems.at[1]),
    ]
    for copy in copies:
        copy.start()
    for copy in copies:
        copy.wait()


def load(rows, counts):
    arrays = (rows, counts)
    held = sum(array.size * array.dtype.itemsize for array in arrays)
    return pl.pallas_call(
        load_kernel,
        out_shape=[jax.ShapeDtypeStruct(array.shape, array.dtype) for array in arrays],
        in_specs=[pl.BlockSpec(memory_space=pl.ANY)] * 2,
        out_specs=[pl.BlockSpec(memory_space=pltpu.VMEM)] * 2,
        scratch_shapes=[pltpu.SemaphoreType.DMA((2,))],
        cost_estimate=pl.CostEstimate(flops=0, bytes_accessed=4 * held, transcendentals=0),
        compiler_params=pltpu.CompilerParams(vmem_limit_bytes=VMEM_WHOLE - VMEM_ROOM - held),
    )(*arrays)


def sum_kernel(parts_ref, out_ref):
    total = parts_ref[0]
    for n in range(1, parts_ref.shape[0]):
        total = total + parts_ref[n]
    out_ref[...] = total


def sum_of(parts):
    vmem = pl.BlockSpec(memory_space=pltpu.VMEM)
    return pl.pallas_call(
        sum_kernel,
        out_shape=jax.ShapeDtypeStruct(parts.shape[1:], parts.dtype),
        in_specs=[vmem],
        out_specs=vmem,
        compiler_params=pltpu.CompilerParams(vmem_limit_bytes=VMEM_BYTES),
    )(parts)


def standard_rows(rows, totals, people_all):
    freq = (totals.astype(jnp.float32) + 1.0) / (2.0 * people_all + 2.0)
    scale = 1.0 / jnp.sqrt(2.0 * freq * (1.0 - freq))
    return ((rows.astype(jnp.float32) - 2.0 * freq) * scale).astype(jnp.bfloat16)


def scaled_product(one, other):
    dims = (((1,), (1,)), ((), ()))
    out = lax.dot_general(one, other, dims, preferred_element_type=jnp.float32)
    return (out / math.sqrt(one.shape[1])).astype(jnp.bfloat16)


def early_kernel(count, people_all, *refs):
    (direct_ref, crossed_ref), rows, outs = refs[:2], refs[2 : count + 2], refs[count + 2 :]
    for n in range(count):
        totals_ref = crossed_ref if n == count - 1 else direct_ref
        outs[n][...] = standard_rows(rows[n][...], totals_ref[...], people_all)


def standardize(people_all, direct, crossed, wide, single):
    rows = [*wide, single]
    vmem = pl.BlockSpec(memory_space=pltpu.VMEM)
    return pl.pallas_call(
        functools.partial(early_kernel, len(rows), people_all),
        out_shape=[jax.ShapeDtypeStruct(single.shape, single.dtype)] * len(rows),
        in_specs=[vmem] * (2 + len(rows)),
        out_specs=[vmem] * len(rows),
        compiler_params=pltpu.CompilerParams(vmem_limit_bytes=VMEM_BYTES),
    )(direct, crossed, *rows)


def late_kernel(half, people_all, role_ref, *refs):
    direct_ref, crossed_ref, passed_ref = refs[:3]
    standard, relayed = refs[3 : half + 4], refs[half + 4 : 2 * half + 3]
    outs, (wide_ref, all_ref) = refs[2 * half + 3 : -2], refs[-2:]
    sent_refs, kept_refs = outs[:half], outs[half:]
    rows = passed_ref.shape[0]

    @pl.when(role_ref[0] == 1)
    def _():
        wide_ref[:rows, :] = standard[0][...]

    @pl.when(role_ref[0] == 0)
    def _():
        wide_ref[:rows, :] = standard_rows(passed_ref[...], direct_ref[...], people_all)

    all_ref[:rows, :] = standard[half][...]
    for t in range(1, half):
        at = slice(t * rows, (t + 1) * rows)
        wide_ref[at, :] = standard[t][...]
        all_ref[at, :] = standard_rows(relayed[t - 1][...], crossed_ref[...], people_all)
    for one, other, outs in ((all_ref, wide_ref, sent_refs), (wide_ref, all_ref, kept_refs)):
        blocks = scaled_product(one[...], other[...])
        for t in range(half):
            outs[t][...] = blocks[t * rows : (t + 1) * rows]


def multiply(role, people_all, direct, crossed, passed, standard, relayed):
    half = len(standard) - 1
    rows, markers = passed.shape
    vmem = pl.BlockSpec(memory_space=pltpu.VMEM)
    outs = pl.pallas_call(
        functools.partial(late_kernel, half, people_all),
        out_shape=[jax.ShapeDtypeStruct((rows, half * rows), jnp.bfloat16)] * (2 * half),
        in_specs=[pl.BlockSpec(memory_space=pltpu.SMEM)] + [vmem] * (3 + 2 * half),
        out_specs=[vmem] * (2 * half),
        scratch_shapes=[pltpu.VMEM((half * rows, markers), jnp.bfloat16)] * 2,
        compiler_params=pltpu.CompilerParams(vmem_limit_bytes=VMEM_BYTES),
    )(role, direct, crossed, passed, *standard, *relayed)
    return list(outs[:half]), list(outs[half:])


def place_kernel(half, role_ref, *refs):
    sent, kept, out_ref = refs[:half], refs[half:-1], refs[-1]
    rows = out_ref.shape[1]
    place = role_ref[1]
    near = 2 * half

    def put(block, part, column):
        to = pl.ds(pl.multiple_of(block * rows, rows), rows)
        out_ref[0, :, to] = part[:, column * rows : (column + 1) * rows]

    @pl.when(role_ref[0] == 1)
    def _():
        for t in range(half):
            for part, chip in ((kept[t], place ^ 2 * t), (sent[t], place ^ 2 * t + 1)):
                for m in range(half):
                    put(chip ^ near * m, part, m)

    @pl.when(role_ref[0] == 0)
    def _():
        for t in range(half):
            chip = place ^ near * t
            for d in range(half):
                put(chip ^ 2 * d, sent[t], d)
                put(chip ^ 2 * d + 1, kept[t], d)


def place_blocks(role, half, sent, kept):
    rows = sent[0].shape[0]
    vmem = pl.BlockSpec(memory_space=pltpu.VMEM)
    return pl.pallas_call(
        functools.partial(place_kernel, half),
        out_shape=jax.ShapeDtypeStruct((1, rows, 2 * half * half * rows), jnp.bfloat16),
        in_specs=[pl.BlockSpec(memory_space=pltpu.SMEM)] + [vmem] * (2 * half),
        out_specs=vmem,
        compiler_params=pltpu.CompilerParams(vmem_limit_bytes=VMEM_BYTES),
    )(role, *sent, *kept)


def one_round(round_number, cohorts, blocks, own, counts):
    half = half_size(blocks)
    near = 2 * half
    left = left_cohorts(cohorts, round_number)

    def send(value, *legs):
        pairs = []
        for c in left:
            for i in range(blocks):
                for leg in legs:
                    (c0, i0), (c1, i1) = leg(c, i)
                    pairs.append((c0 * blocks + i0, c1 * blocks + i1))
        return lax.ppermute(value, AXES, pairs)

    def left_to_left(d):
        return lambda c, i: ((c, i), (c, i ^ d))

    def left_to_mate(d):
        return lambda c, i: ((c, i), (c ^ 1, i ^ d))

    def mate_to_left(d):
        return lambda c, i: ((c ^ 1, i), (c, i ^ d))

    def mate_to_mate(d):
        return lambda c, i: ((c ^ 1, i), (c ^ 1, i ^ d))

    def owner_to_left(c, i):
        return (c ^ round_number, i), (c, i)

    def owner_to_mate(c, i):
        return (c ^ round_number, i), (c ^ 1, i)

    def right_rows_to_mate(t):
        return lambda c, i: ((c ^ 1, i), (c ^ round_number, i ^ near * t))

    def right_rows_to_left(c, i):
        return (c, i), (c ^ 1 ^ round_number, i)

    def left_to_owner(t):
        return lambda c, i: ((c, i), (c ^ round_number, i ^ near * t))

    def mate_to_owner(t):
        return lambda c, i: ((c ^ 1, i), (c ^ round_number, i ^ near * t))

    cohort = lax.axis_index("cohort")
    is_left = functools.reduce(jnp.logical_or, [cohort == c for c in left])
    role = jnp.stack([is_left.astype(jnp.int32), lax.axis_index("person")])

    first = [own] + [
        send(own, left_to_left(2 * t), right_rows_to_mate(t)) for t in range(1, half)
    ]
    beside = send(own, left_to_mate(0), mate_to_left(0))
    second = [send(beside, right_rows_to_left, mate_to_mate(1))]
    counts, _ = lax.optimization_barrier((counts, beside))
    spread = jnp.broadcast_to(counts[None], (blocks, *counts.shape))
    totals = sum_of(lax.all_to_all(spread, "person", 0, 0, tiled=True))
    *first[1:], totals = lax.optimization_barrier((*first[1:], totals))
    second += [send(first[t], left_to_mate(1), mate_to_left(0)) for t in range(1, half)]
    passed = send(second[0], left_to_mate(0), mate_to_left(0))
    crossed = send(totals, left_to_mate(0), owner_to_left)
    direct = totals
    if round_number != 1:
        direct = send(totals, left_to_left(0), owner_to_mate)
    people_all = own.shape[0] * blocks
    standard = standardize(people_all, direct, crossed, first, second[0])
    sent, kept = multiply(role, people_all, direct, crossed, passed, standard, second[1:])
    sent[-1] = send(sent[-1], mate_to_left(2 * half - 1), left_to_owner(half - 1))
    if round_number != 1:
        kept[0] = send(kept[0], left_to_left(0), mate_to_owner(0))
    for t in reversed(range(1, half)):
        kept[t] = send(kept[t], left_to_left(2 * t), mate_to_owner(t))
        sent[t - 1] = send(sent[t - 1], mate_to_left(2 * t - 1), left_to_owner(t - 1))
    return place_blocks(role, half, sent, kept)


def on_device(dosages, allele_counts, partner):
    cohorts, blocks = lax.axis_size("cohort"), lax.axis_size("person")
    rounds = [
        functools.partial(one_round, round_number, cohorts, blocks)
        for round_number in range(1, cohorts)
    ]
    return lax.switch(partner[0] - 1, rounds, *load(dosages[0], allele_counts[0]))


def solution(mesh):
    placed = (P("cohort", "person", None), P("cohort", "person", None), P())
    return jax.shard_map(
        on_device,
        mesh=mesh,
        in_specs=placed,
        out_specs=P("cohort", "person", None),
        check_vma=False,
    )
```

```python
import functools
import math

import jax
import jax.numpy as jnp
from jax import lax
from jax.experimental import pallas as pl
from jax.experimental.pallas import tpu as pltpu
from jax.sharding import PartitionSpec as P

AXES = ("cohort", "person")
VMEM_BYTES = 48 * 1024 * 1024
VMEM_WHOLE = 64 * 1024 * 1024
VMEM_ROOM = 128 * 1024


def left_cohorts(cohorts, round_number):
    if round_number == 1:
        return [c for c in range(cohorts) if c & 1 == 0]
    top = 1 << (round_number.bit_length() - 1)
    return [
        c
        for c in range(cohorts)
        if (c & top == 0 and c & 1 == 0) or (c & top and (c ^ round_number ^ 1) & 1 == 0)
    ]


def half_size(blocks):
    return 1 << (blocks.bit_length() // 2 - 1)


def load_kernel(count, *refs):
    sources, targets, sems = refs[:count], refs[count:-1], refs[-1]
    copies = [
        pltpu.make_async_copy(source, target, sems.at[n])
        for n, (source, target) in enumerate(zip(sources, targets))
    ]
    for copy in copies:
        copy.start()
    for copy in copies:
        copy.wait()


def load(*arrays):
    held = sum(array.size * array.dtype.itemsize for array in arrays)
    return pl.pallas_call(
        functools.partial(load_kernel, len(arrays)),
        out_shape=[pltpu.VMEM(array.shape, array.dtype) for array in arrays],
        in_specs=[pl.BlockSpec(memory_space=pl.ANY)] * len(arrays),
        out_specs=[pl.BlockSpec(memory_space=pltpu.VMEM)] * len(arrays),
        scratch_shapes=[pltpu.SemaphoreType.DMA((len(arrays),))],
        compiler_params=pltpu.CompilerParams(vmem_limit_bytes=VMEM_WHOLE - VMEM_ROOM - held),
    )(*arrays)


def sum_kernel(parts_ref, out_ref):
    total = parts_ref[0]
    for n in range(1, parts_ref.shape[0]):
        total = total + parts_ref[n]
    out_ref[...] = total


def sum_of(parts):
    vmem = pl.BlockSpec(memory_space=pltpu.VMEM)
    return pl.pallas_call(
        sum_kernel,
        out_shape=jax.ShapeDtypeStruct(parts.shape[1:], parts.dtype),
        in_specs=[vmem],
        out_specs=vmem,
        compiler_params=pltpu.CompilerParams(vmem_limit_bytes=VMEM_BYTES),
    )(parts)


def standard_rows(rows, totals, people_all):
    freq = (totals.astype(jnp.float32) + 1.0) / (2.0 * people_all + 2.0)
    scale = 1.0 / jnp.sqrt(2.0 * freq * (1.0 - freq))
    return ((rows.astype(jnp.float32) - 2.0 * freq) * scale).astype(jnp.bfloat16)


def scaled_product(one, other):
    dims = (((1,), (1,)), ((), ()))
    out = lax.dot_general(one, other, dims, preferred_element_type=jnp.float32)
    return (out / math.sqrt(one.shape[1])).astype(jnp.bfloat16)


def early_kernel(count, people_all, *refs):
    (direct_ref, crossed_ref), rows, outs = refs[:2], refs[2 : count + 2], refs[count + 2 :]
    for n in range(count):
        totals_ref = crossed_ref if n == count - 1 else direct_ref
        outs[n][...] = standard_rows(rows[n][...], totals_ref[...], people_all)


def standardize(people_all, direct, crossed, wide, single):
    rows = [*wide, single]
    vmem = pl.BlockSpec(memory_space=pltpu.VMEM)
    return pl.pallas_call(
        functools.partial(early_kernel, len(rows), people_all),
        out_shape=[jax.ShapeDtypeStruct(single.shape, single.dtype)] * len(rows),
        in_specs=[vmem] * (2 + len(rows)),
        out_specs=[vmem] * len(rows),
        compiler_params=pltpu.CompilerParams(vmem_limit_bytes=VMEM_BYTES),
    )(direct, crossed, *rows)


def late_kernel(half, people_all, role_ref, *refs):
    direct_ref, crossed_ref, passed_ref = refs[:3]
    standard, relayed = refs[3 : half + 4], refs[half + 4 : 2 * half + 3]
    outs, (wide_ref, all_ref) = refs[2 * half + 3 : -2], refs[-2:]
    sent_refs, kept_refs = outs[:half], outs[half:]
    rows = passed_ref.shape[0]

    @pl.when(role_ref[0] == 1)
    def _():
        wide_ref[:rows, :] = standard[0][...]

    @pl.when(role_ref[0] == 0)
    def _():
        wide_ref[:rows, :] = standard_rows(passed_ref[...], direct_ref[...], people_all)

    all_ref[:rows, :] = standard[half][...]
    for t in range(1, half):
        at = slice(t * rows, (t + 1) * rows)
        wide_ref[at, :] = standard[t][...]
        all_ref[at, :] = standard_rows(relayed[t - 1][...], crossed_ref[...], people_all)
    for one, other, outs in ((all_ref, wide_ref, sent_refs), (wide_ref, all_ref, kept_refs)):
        blocks = scaled_product(one[...], other[...])
        for t in range(half):
            outs[t][...] = blocks[t * rows : (t + 1) * rows]


def multiply(role, people_all, direct, crossed, passed, standard, relayed):
    half = len(standard) - 1
    rows, markers = passed.shape
    vmem = pl.BlockSpec(memory_space=pltpu.VMEM)
    outs = pl.pallas_call(
        functools.partial(late_kernel, half, people_all),
        out_shape=[jax.ShapeDtypeStruct((rows, half * rows), jnp.bfloat16)] * (2 * half),
        in_specs=[pl.BlockSpec(memory_space=pltpu.SMEM)] + [vmem] * (3 + 2 * half),
        out_specs=[vmem] * (2 * half),
        scratch_shapes=[pltpu.VMEM((half * rows, markers), jnp.bfloat16)] * 2,
        compiler_params=pltpu.CompilerParams(vmem_limit_bytes=VMEM_BYTES),
    )(role, direct, crossed, passed, *standard, *relayed)
    return list(outs[:half]), list(outs[half:])


def place_kernel(half, role_ref, *refs):
    sent, kept, (out_ref, sems) = refs[:half], refs[half : 2 * half], refs[2 * half :]
    rows = out_ref.shape[1]
    place = role_ref[1]
    near = 2 * half

    def run(blocks):
        copies = []
        for n, (block, part, column) in enumerate(blocks):
            to = pl.ds(pl.multiple_of(block * rows, rows), rows)
            source = part.at[:, pl.ds(column * rows, rows)]
            copies.append(pltpu.make_async_copy(source, out_ref.at[0, :, to], sems.at[n]))
        for copy in copies:
            copy.start()
        for copy in copies:
            copy.wait()

    @pl.when(role_ref[0] == 1)
    def _():
        blocks = []
        for t in range(half):
            for part, chip in ((kept[t], place ^ 2 * t), (sent[t], place ^ 2 * t + 1)):
                blocks += [(chip ^ near * m, part, m) for m in range(half)]
        run(blocks)

    @pl.when(role_ref[0] == 0)
    def _():
        blocks = []
        for t in range(half):
            chip = place ^ near * t
            for d in range(half):
                blocks += [(chip ^ 2 * d, sent[t], d), (chip ^ 2 * d + 1, kept[t], d)]
        run(blocks)


def place_blocks(role, half, sent, kept):
    rows = sent[0].shape[0]
    vmem = pl.BlockSpec(memory_space=pltpu.VMEM)
    return pl.pallas_call(
        functools.partial(place_kernel, half),
        out_shape=pltpu.HBM((1, rows, 2 * half * half * rows), jnp.bfloat16),
        in_specs=[pl.BlockSpec(memory_space=pltpu.SMEM)] + [vmem] * (2 * half),
        out_specs=pl.BlockSpec(memory_space=pltpu.HBM),
        scratch_shapes=[pltpu.SemaphoreType.DMA((2 * half * half,))],
        compiler_params=pltpu.CompilerParams(vmem_limit_bytes=VMEM_BYTES),
    )(role, *sent, *kept)


def one_round(round_number, cohorts, blocks, own, counts):
    half = half_size(blocks)
    near = 2 * half
    left = left_cohorts(cohorts, round_number)

    def send(value, *legs):
        pairs = []
        for c in left:
            for i in range(blocks):
                for leg in legs:
                    (c0, i0), (c1, i1) = leg(c, i)
                    pairs.append((c0 * blocks + i0, c1 * blocks + i1))
        return lax.ppermute(value, AXES, pairs)

    def left_to_left(d):
        return lambda c, i: ((c, i), (c, i ^ d))

    def left_to_mate(d):
        return lambda c, i: ((c, i), (c ^ 1, i ^ d))

    def mate_to_left(d):
        return lambda c, i: ((c ^ 1, i), (c, i ^ d))

    def mate_to_mate(d):
        return lambda c, i: ((c ^ 1, i), (c ^ 1, i ^ d))

    def owner_to_left(c, i):
        return (c ^ round_number, i), (c, i)

    def owner_to_mate(c, i):
        return (c ^ round_number, i), (c ^ 1, i)

    def right_rows_to_mate(t):
        return lambda c, i: ((c ^ 1, i), (c ^ round_number, i ^ near * t))

    def right_rows_to_left(c, i):
        return (c, i), (c ^ 1 ^ round_number, i)

    def left_to_owner(t):
        return lambda c, i: ((c, i), (c ^ round_number, i ^ near * t))

    def mate_to_owner(t):
        return lambda c, i: ((c ^ 1, i), (c ^ round_number, i ^ near * t))

    cohort = lax.axis_index("cohort")
    is_left = functools.reduce(jnp.logical_or, [cohort == c for c in left])
    role = jnp.stack([is_left.astype(jnp.int32), lax.axis_index("person")])

    first = [own] + [
        send(own, left_to_left(2 * t), right_rows_to_mate(t)) for t in range(1, half)
    ]
    beside = send(own, left_to_mate(0), mate_to_left(0))
    second = [send(beside, right_rows_to_left, mate_to_mate(1))]
    counts, _ = lax.optimization_barrier((counts, beside))
    spread = jnp.broadcast_to(counts[None], (blocks, *counts.shape))
    totals = sum_of(lax.all_to_all(spread, "person", 0, 0, tiled=True))
    *first[1:], totals = lax.optimization_barrier((*first[1:], totals))
    second += [send(first[t], left_to_mate(1), mate_to_left(0)) for t in range(1, half)]
    passed = send(second[0], left_to_mate(0), mate_to_left(0))
    crossed = send(totals, left_to_mate(0), owner_to_left)
    direct = totals
    if round_number != 1:
        direct = send(totals, left_to_left(0), owner_to_mate)
    people_all = own.shape[0] * blocks
    standard = standardize(people_all, direct, crossed, first, second[0])
    sent, kept = multiply(role, people_all, direct, crossed, passed, standard, second[1:])
    sent[-1] = send(sent[-1], mate_to_left(2 * half - 1), left_to_owner(half - 1))
    if round_number != 1:
        kept[0] = send(kept[0], left_to_left(0), mate_to_owner(0))
    for t in reversed(range(1, half)):
        kept[t] = send(kept[t], left_to_left(2 * t), mate_to_owner(t))
        sent[t - 1] = send(sent[t - 1], mate_to_left(2 * t - 1), left_to_owner(t - 1))
    return place_blocks(role, half, sent, kept)


def on_device(dosages, allele_counts, partner):
    cohorts, blocks = lax.axis_size("cohort"), lax.axis_size("person")
    rounds = [
        functools.partial(one_round, round_number, cohorts, blocks)
        for round_number in range(1, cohorts)
    ]
    own, counts, partner = load(dosages[0], allele_counts[0], partner)
    return lax.switch(partner[0] - 1, rounds, own, counts)


def solution(mesh):
    placed = (P("cohort", "person", None), P("cohort", "person", None), P())
    return jax.shard_map(
        on_device,
        mesh=mesh,
        in_specs=placed,
        out_specs=P("cohort", "person", None),
        check_vma=False,
    )
```

```python
import functools
import math

import jax
import jax.numpy as jnp
from jax import lax
from jax.experimental import pallas as pl
from jax.experimental.pallas import tpu as pltpu
from jax.sharding import PartitionSpec as P

AXES = ("cohort", "person")
VMEM_BYTES = 48 * 1024 * 1024
VMEM_WHOLE = 64 * 1024 * 1024
VMEM_ROOM = 128 * 1024


def left_cohorts(cohorts, round_number):
    if round_number == 1:
        return [c for c in range(cohorts) if c & 1 == 0]
    top = 1 << (round_number.bit_length() - 1)
    return [
        c
        for c in range(cohorts)
        if (c & top == 0 and c & 1 == 0) or (c & top and (c ^ round_number ^ 1) & 1 == 0)
    ]


def half_size(blocks):
    return 1 << (blocks.bit_length() // 2 - 1)


def load_kernel(count, *refs):
    sources, targets, sems = refs[:count], refs[count:-1], refs[-1]
    copies = [
        pltpu.make_async_copy(source, target, sems.at[n])
        for n, (source, target) in enumerate(zip(sources, targets))
    ]
    for copy in copies:
        copy.start()
    for copy in copies:
        copy.wait()


def load(*arrays):
    held = sum(array.size * array.dtype.itemsize for array in arrays)
    return pl.pallas_call(
        functools.partial(load_kernel, len(arrays)),
        out_shape=[pltpu.VMEM(array.shape, array.dtype) for array in arrays],
        in_specs=[pl.BlockSpec(memory_space=pl.ANY)] * len(arrays),
        out_specs=[pl.BlockSpec(memory_space=pltpu.VMEM)] * len(arrays),
        scratch_shapes=[pltpu.SemaphoreType.DMA((len(arrays),))],
        compiler_params=pltpu.CompilerParams(vmem_limit_bytes=VMEM_WHOLE - VMEM_ROOM - held),
    )(*arrays)


def sum_kernel(parts_ref, out_ref):
    total = parts_ref[0]
    for n in range(1, parts_ref.shape[0]):
        total = total + parts_ref[n]
    out_ref[...] = total


def sum_of(parts):
    vmem = pl.BlockSpec(memory_space=pltpu.VMEM)
    return pl.pallas_call(
        sum_kernel,
        out_shape=jax.ShapeDtypeStruct(parts.shape[1:], parts.dtype),
        in_specs=[vmem],
        out_specs=vmem,
        compiler_params=pltpu.CompilerParams(vmem_limit_bytes=VMEM_BYTES),
    )(parts)


def standard_rows(rows, totals, people_all):
    freq = (totals.astype(jnp.float32) + 1.0) / (2.0 * people_all + 2.0)
    scale = 1.0 / jnp.sqrt(2.0 * freq * (1.0 - freq))
    return ((rows.astype(jnp.float32) - 2.0 * freq) * scale).astype(jnp.bfloat16)


def scaled_product(one, other):
    dims = (((1,), (1,)), ((), ()))
    out = lax.dot_general(one, other, dims, preferred_element_type=jnp.float32)
    return (out / math.sqrt(one.shape[1])).astype(jnp.bfloat16)


def early_kernel(count, people_all, *refs):
    (direct_ref, crossed_ref), rows, outs = refs[:2], refs[2 : count + 2], refs[count + 2 :]
    for n in range(count):
        totals_ref = crossed_ref if n == count - 1 else direct_ref
        outs[n][...] = standard_rows(rows[n][...], totals_ref[...], people_all)


def standardize(people_all, direct, crossed, wide, single):
    rows = [*wide, single]
    vmem = pl.BlockSpec(memory_space=pltpu.VMEM)
    return pl.pallas_call(
        functools.partial(early_kernel, len(rows), people_all),
        out_shape=[jax.ShapeDtypeStruct(single.shape, single.dtype)] * len(rows),
        in_specs=[vmem] * (2 + len(rows)),
        out_specs=[vmem] * len(rows),
        compiler_params=pltpu.CompilerParams(vmem_limit_bytes=VMEM_BYTES),
    )(direct, crossed, *rows)


def late_kernel(half, people_all, role_ref, *refs):
    direct_ref, crossed_ref, passed_ref = refs[:3]
    standard, relayed = refs[3 : half + 4], refs[half + 4 : 2 * half + 3]
    outs, (wide_ref, all_ref) = refs[2 * half + 3 : -2], refs[-2:]
    sent_refs, kept_refs = outs[:half], outs[half:]
    rows = passed_ref.shape[0]

    @pl.when(role_ref[0] == 1)
    def _():
        wide_ref[:rows, :] = standard[0][...]

    @pl.when(role_ref[0] == 0)
    def _():
        wide_ref[:rows, :] = standard_rows(passed_ref[...], direct_ref[...], people_all)

    all_ref[:rows, :] = standard[half][...]
    for t in range(1, half):
        at = slice(t * rows, (t + 1) * rows)
        wide_ref[at, :] = standard[t][...]
        all_ref[at, :] = standard_rows(relayed[t - 1][...], crossed_ref[...], people_all)
    for one, other, outs in ((all_ref, wide_ref, sent_refs), (wide_ref, all_ref, kept_refs)):
        blocks = scaled_product(one[...], other[...])
        for t in range(half):
            outs[t][...] = blocks[t * rows : (t + 1) * rows]


def multiply(role, people_all, direct, crossed, passed, standard, relayed):
    half = len(standard) - 1
    rows, markers = passed.shape
    vmem = pl.BlockSpec(memory_space=pltpu.VMEM)
    outs = pl.pallas_call(
        functools.partial(late_kernel, half, people_all),
        out_shape=[jax.ShapeDtypeStruct((rows, half * rows), jnp.bfloat16)] * (2 * half),
        in_specs=[pl.BlockSpec(memory_space=pltpu.SMEM)] + [vmem] * (3 + 2 * half),
        out_specs=[vmem] * (2 * half),
        scratch_shapes=[pltpu.VMEM((half * rows, markers), jnp.bfloat16)] * 2,
        compiler_params=pltpu.CompilerParams(vmem_limit_bytes=VMEM_BYTES),
    )(role, direct, crossed, passed, *standard, *relayed)
    return list(outs[:half]), list(outs[half:])


def place_kernel(half, role_ref, *refs):
    sent, kept, (out_ref, sems) = refs[:half], refs[half : 2 * half], refs[2 * half :]
    rows = out_ref.shape[1]
    place = role_ref[1]
    near = 2 * half

    def run(blocks):
        copies = []
        for n, (block, part, column) in enumerate(blocks):
            to = pl.ds(pl.multiple_of(block * rows, rows), rows)
            source = part.at[:, pl.ds(column * rows, rows)]
            copies.append(pltpu.make_async_copy(source, out_ref.at[0, :, to], sems.at[n]))
        for copy in copies:
            copy.start()
        for copy in copies:
            copy.wait()

    @pl.when(role_ref[0] == 1)
    def _():
        blocks = []
        for t in range(half):
            for part, chip in ((kept[t], place ^ 2 * t), (sent[t], place ^ 2 * t + 1)):
                blocks += [(chip ^ near * m, part, m) for m in range(half)]
        run(blocks)

    @pl.when(role_ref[0] == 0)
    def _():
        blocks = []
        for t in range(half):
            chip = place ^ near * t
            for d in range(half):
                blocks += [(chip ^ 2 * d, sent[t], d), (chip ^ 2 * d + 1, kept[t], d)]
        run(blocks)


def place_blocks(role, half, sent, kept):
    rows = sent[0].shape[0]
    vmem = pl.BlockSpec(memory_space=pltpu.VMEM)
    return pl.pallas_call(
        functools.partial(place_kernel, half),
        out_shape=pltpu.HBM((1, rows, 2 * half * half * rows), jnp.bfloat16),
        in_specs=[pl.BlockSpec(memory_space=pltpu.SMEM)] + [vmem] * (2 * half),
        out_specs=pl.BlockSpec(memory_space=pltpu.HBM),
        scratch_shapes=[pltpu.SemaphoreType.DMA((2 * half * half,))],
        compiler_params=pltpu.CompilerParams(vmem_limit_bytes=VMEM_BYTES),
    )(role, *sent, *kept)


def one_round(round_number, cohorts, blocks, own, beside, totals):
    half = half_size(blocks)
    near = 2 * half
    left = left_cohorts(cohorts, round_number)

    def send(value, *legs):
        pairs = []
        for c in left:
            for i in range(blocks):
                for leg in legs:
                    (c0, i0), (c1, i1) = leg(c, i)
                    pairs.append((c0 * blocks + i0, c1 * blocks + i1))
        return lax.ppermute(value, AXES, pairs)

    def left_to_left(d):
        return lambda c, i: ((c, i), (c, i ^ d))

    def left_to_mate(d):
        return lambda c, i: ((c, i), (c ^ 1, i ^ d))

    def mate_to_left(d):
        return lambda c, i: ((c ^ 1, i), (c, i ^ d))

    def mate_to_mate(d):
        return lambda c, i: ((c ^ 1, i), (c ^ 1, i ^ d))

    def owner_to_left(c, i):
        return (c ^ round_number, i), (c, i)

    def owner_to_mate(c, i):
        return (c ^ round_number, i), (c ^ 1, i)

    def right_rows_to_mate(t):
        return lambda c, i: ((c ^ 1, i), (c ^ round_number, i ^ near * t))

    def right_rows_to_left(c, i):
        return (c, i), (c ^ 1 ^ round_number, i)

    def left_to_owner(t):
        return lambda c, i: ((c, i), (c ^ round_number, i ^ near * t))

    def mate_to_owner(t):
        return lambda c, i: ((c ^ 1, i), (c ^ round_number, i ^ near * t))

    cohort = lax.axis_index("cohort")
    is_left = functools.reduce(jnp.logical_or, [cohort == c for c in left])
    role = jnp.stack([is_left.astype(jnp.int32), lax.axis_index("person")])

    first = [own] + [
        send(own, left_to_left(2 * t), right_rows_to_mate(t)) for t in range(1, half)
    ]
    second = [send(beside, right_rows_to_left, mate_to_mate(1))]
    crossed = send(totals, left_to_mate(0), owner_to_left)
    direct = totals
    if round_number != 1:
        direct = send(totals, left_to_left(0), owner_to_mate)
    *first[1:], direct, crossed = lax.optimization_barrier((*first[1:], direct, crossed))
    second += [send(first[t], left_to_mate(1), mate_to_left(0)) for t in range(1, half)]
    people_all = own.shape[0] * blocks
    standard = standardize(people_all, direct, crossed, first, second[0])
    second[0], *standard = lax.optimization_barrier((second[0], *standard))
    passed = send(second[0], left_to_mate(0), mate_to_left(0))
    sent, kept = multiply(role, people_all, direct, crossed, passed, standard, second[1:])
    sent[-1] = send(sent[-1], mate_to_left(2 * half - 1), left_to_owner(half - 1))
    if round_number != 1:
        kept[0] = send(kept[0], left_to_left(0), mate_to_owner(0))
    for t in reversed(range(1, half)):
        kept[t] = send(kept[t], left_to_left(2 * t), mate_to_owner(t))
        sent[t - 1] = send(sent[t - 1], mate_to_left(2 * t - 1), left_to_owner(t - 1))
    return place_blocks(role, half, sent, kept)


def on_device(dosages, allele_counts, partner):
    cohorts, blocks = lax.axis_size("cohort"), lax.axis_size("person")
    rounds = [
        functools.partial(one_round, round_number, cohorts, blocks)
        for round_number in range(1, cohorts)
    ]
    own, counts, partner = load(dosages[0], allele_counts[0], partner)
    beside = lax.ppermute(own, "cohort", [(c, c ^ 1) for c in range(cohorts)])
    spread = jnp.broadcast_to(counts[None], (blocks, *counts.shape))
    totals = sum_of(lax.all_to_all(spread, "person", 0, 0, tiled=True))
    return lax.switch(partner[0] - 1, rounds, own, beside, totals)


def solution(mesh):
    placed = (P("cohort", "person", None), P("cohort", "person", None), P())
    return jax.shard_map(
        on_device,
        mesh=mesh,
        in_specs=placed,
        out_specs=P("cohort", "person", None),
        check_vma=False,
    )
```

```python
import functools
import math

import jax
import jax.numpy as jnp
from jax import lax
from jax.experimental import pallas as pl
from jax.experimental.pallas import tpu as pltpu
from jax.sharding import PartitionSpec as P

AXES = ("cohort", "person")
VMEM_BYTES = 48 * 1024 * 1024
VMEM_WHOLE = 64 * 1024 * 1024
VMEM_ROOM = 128 * 1024


def left_cohorts(cohorts, round_number):
    if round_number == 1:
        return [c for c in range(cohorts) if c & 1 == 0]
    top = 1 << (round_number.bit_length() - 1)
    return [
        c
        for c in range(cohorts)
        if (c & top == 0 and c & 1 == 0) or (c & top and (c ^ round_number ^ 1) & 1 == 0)
    ]


def half_size(blocks):
    return 1 << (blocks.bit_length() // 2 - 1)


def load_kernel(count, *refs):
    sources, targets, sems = refs[:count], refs[count:-1], refs[-1]
    copies = [
        pltpu.make_async_copy(source, target, sems.at[n])
        for n, (source, target) in enumerate(zip(sources, targets))
    ]
    for copy in copies:
        copy.start()
    for copy in copies:
        copy.wait()


def load(*arrays):
    held = sum(array.size * array.dtype.itemsize for array in arrays)
    return pl.pallas_call(
        functools.partial(load_kernel, len(arrays)),
        out_shape=[pltpu.VMEM(array.shape, array.dtype) for array in arrays],
        in_specs=[pl.BlockSpec(memory_space=pl.ANY)] * len(arrays),
        out_specs=[pl.BlockSpec(memory_space=pltpu.VMEM)] * len(arrays),
        scratch_shapes=[pltpu.SemaphoreType.DMA((len(arrays),))],
        compiler_params=pltpu.CompilerParams(vmem_limit_bytes=VMEM_WHOLE - VMEM_ROOM - held),
    )(*arrays)


def sum_kernel(parts_ref, out_ref):
    total = parts_ref[0]
    for n in range(1, parts_ref.shape[0]):
        total = total + parts_ref[n]
    out_ref[...] = total


def sum_of(parts):
    vmem = pl.BlockSpec(memory_space=pltpu.VMEM)
    return pl.pallas_call(
        sum_kernel,
        out_shape=jax.ShapeDtypeStruct(parts.shape[1:], parts.dtype),
        in_specs=[vmem],
        out_specs=vmem,
        compiler_params=pltpu.CompilerParams(vmem_limit_bytes=VMEM_BYTES),
    )(parts)


def standard_rows(rows, totals, people_all):
    freq = (totals.astype(jnp.float32) + 1.0) / (2.0 * people_all + 2.0)
    scale = 1.0 / jnp.sqrt(2.0 * freq * (1.0 - freq))
    return ((rows.astype(jnp.float32) - 2.0 * freq) * scale).astype(jnp.bfloat16)


def early_kernel(count, people_all, *refs):
    (direct_ref, crossed_ref), rows, outs = refs[:2], refs[2 : count + 2], refs[count + 2 :]
    for n in range(count):
        totals_ref = crossed_ref if n == count - 1 else direct_ref
        outs[n][...] = standard_rows(rows[n][...], totals_ref[...], people_all)


def standardize(people_all, direct, crossed, wide, single):
    rows = [*wide, single]
    vmem = pl.BlockSpec(memory_space=pltpu.VMEM)
    return pl.pallas_call(
        functools.partial(early_kernel, len(rows), people_all),
        out_shape=[jax.ShapeDtypeStruct(single.shape, single.dtype)] * len(rows),
        in_specs=[vmem] * (2 + len(rows)),
        out_specs=[vmem] * len(rows),
        compiler_params=pltpu.CompilerParams(vmem_limit_bytes=VMEM_BYTES),
    )(direct, crossed, *rows)


def late_kernel(half, people_all, role_ref, *refs):
    direct_ref, crossed_ref, passed_ref = refs[:3]
    standard, relayed = refs[3 : half + 4], refs[half + 4 : 2 * half + 3]
    outs, (wide_ref, all_ref) = refs[2 * half + 3 : -2], refs[-2:]
    sent_refs, kept_refs = outs[:half], outs[half:]
    rows = passed_ref.shape[0]

    @pl.when(role_ref[0] == 1)
    def _():
        wide_ref[:rows, :] = standard[0][...]

    @pl.when(role_ref[0] == 0)
    def _():
        wide_ref[:rows, :] = standard_rows(passed_ref[...], direct_ref[...], people_all)

    all_ref[:rows, :] = standard[half][...]
    for t in range(1, half):
        at = slice(t * rows, (t + 1) * rows)
        wide_ref[at, :] = standard[t][...]
        all_ref[at, :] = standard_rows(relayed[t - 1][...], crossed_ref[...], people_all)
    dims = (((1,), (1,)), ((), ()))
    product = lax.dot_general(
        all_ref[...], wide_ref[...], dims, preferred_element_type=jnp.float32
    ) / math.sqrt(passed_ref.shape[1])
    for blocks, parts in ((product, sent_refs), (product.T, kept_refs)):
        for t in range(half):
            parts[t][...] = blocks[t * rows : (t + 1) * rows].astype(jnp.bfloat16)


def multiply(role, people_all, direct, crossed, passed, standard, relayed):
    half = len(standard) - 1
    rows, markers = passed.shape
    vmem = pl.BlockSpec(memory_space=pltpu.VMEM)
    outs = pl.pallas_call(
        functools.partial(late_kernel, half, people_all),
        out_shape=[jax.ShapeDtypeStruct((rows, half * rows), jnp.bfloat16)] * (2 * half),
        in_specs=[pl.BlockSpec(memory_space=pltpu.SMEM)] + [vmem] * (3 + 2 * half),
        out_specs=[vmem] * (2 * half),
        scratch_shapes=[pltpu.VMEM((half * rows, markers), jnp.bfloat16)] * 2,
        compiler_params=pltpu.CompilerParams(vmem_limit_bytes=VMEM_BYTES),
    )(role, direct, crossed, passed, *standard, *relayed)
    return list(outs[:half]), list(outs[half:])


def place_kernel(half, role_ref, *refs):
    sent, kept, (out_ref, sems) = refs[:half], refs[half : 2 * half], refs[2 * half :]
    rows = out_ref.shape[1]
    place = role_ref[1]
    near = 2 * half

    def run(blocks):
        copies = []
        for n, (block, part, column) in enumerate(blocks):
            to = pl.ds(pl.multiple_of(block * rows, rows), rows)
            source = part.at[:, pl.ds(column * rows, rows)]
            copies.append(pltpu.make_async_copy(source, out_ref.at[0, :, to], sems.at[n]))
        for copy in copies:
            copy.start()
        for copy in copies:
            copy.wait()

    @pl.when(role_ref[0] == 1)
    def _():
        blocks = []
        for t in range(half):
            for part, chip in ((kept[t], place ^ 2 * t), (sent[t], place ^ 2 * t + 1)):
                blocks += [(chip ^ near * m, part, m) for m in range(half)]
        run(blocks)

    @pl.when(role_ref[0] == 0)
    def _():
        blocks = []
        for t in range(half):
            chip = place ^ near * t
            for d in range(half):
                blocks += [(chip ^ 2 * d, sent[t], d), (chip ^ 2 * d + 1, kept[t], d)]
        run(blocks)


def place_blocks(role, half, sent, kept):
    rows = sent[0].shape[0]
    vmem = pl.BlockSpec(memory_space=pltpu.VMEM)
    return pl.pallas_call(
        functools.partial(place_kernel, half),
        out_shape=pltpu.HBM((1, rows, 2 * half * half * rows), jnp.bfloat16),
        in_specs=[pl.BlockSpec(memory_space=pltpu.SMEM)] + [vmem] * (2 * half),
        out_specs=pl.BlockSpec(memory_space=pltpu.HBM),
        scratch_shapes=[pltpu.SemaphoreType.DMA((2 * half * half,))],
        compiler_params=pltpu.CompilerParams(vmem_limit_bytes=VMEM_BYTES),
    )(role, *sent, *kept)


def one_round(round_number, cohorts, blocks, own, counts):
    half = half_size(blocks)
    near = 2 * half
    left = left_cohorts(cohorts, round_number)

    def send(value, *legs):
        pairs = []
        for c in left:
            for i in range(blocks):
                for leg in legs:
                    (c0, i0), (c1, i1) = leg(c, i)
                    pairs.append((c0 * blocks + i0, c1 * blocks + i1))
        return lax.ppermute(value, AXES, pairs)

    def left_to_left(d):
        return lambda c, i: ((c, i), (c, i ^ d))

    def left_to_mate(d):
        return lambda c, i: ((c, i), (c ^ 1, i ^ d))

    def mate_to_left(d):
        return lambda c, i: ((c ^ 1, i), (c, i ^ d))

    def mate_to_mate(d):
        return lambda c, i: ((c ^ 1, i), (c ^ 1, i ^ d))

    def owner_to_left(c, i):
        return (c ^ round_number, i), (c, i)

    def owner_to_mate(c, i):
        return (c ^ round_number, i), (c ^ 1, i)

    def right_rows_to_mate(t):
        return lambda c, i: ((c ^ 1, i), (c ^ round_number, i ^ near * t))

    def right_rows_to_left(c, i):
        return (c, i), (c ^ 1 ^ round_number, i)

    def left_to_owner(t):
        return lambda c, i: ((c, i), (c ^ round_number, i ^ near * t))

    def mate_to_owner(t):
        return lambda c, i: ((c ^ 1, i), (c ^ round_number, i ^ near * t))

    cohort = lax.axis_index("cohort")
    is_left = functools.reduce(jnp.logical_or, [cohort == c for c in left])
    role = jnp.stack([is_left.astype(jnp.int32), lax.axis_index("person")])

    first = [own] + [
        send(own, left_to_left(2 * t), right_rows_to_mate(t)) for t in range(1, half)
    ]
    beside = send(own, left_to_mate(0), mate_to_left(0))
    second = [send(beside, right_rows_to_left, mate_to_mate(1))]
    counts, _ = lax.optimization_barrier((counts, beside))
    spread = jnp.broadcast_to(counts[None], (blocks, *counts.shape))
    totals = sum_of(lax.all_to_all(spread, "person", 0, 0, tiled=True))
    *first[1:], totals = lax.optimization_barrier((*first[1:], totals))
    second += [send(first[t], left_to_mate(1), mate_to_left(0)) for t in range(1, half)]
    passed = send(second[0], left_to_mate(0), mate_to_left(0))
    crossed = send(totals, left_to_mate(0), owner_to_left)
    direct = totals
    if round_number != 1:
        direct = send(totals, left_to_left(0), owner_to_mate)
    people_all = own.shape[0] * blocks
    standard = standardize(people_all, direct, crossed, first, second[0])
    sent, kept = multiply(role, people_all, direct, crossed, passed, standard, second[1:])
    sent[-1] = send(sent[-1], mate_to_left(2 * half - 1), left_to_owner(half - 1))
    if round_number == 1:
        kept[-1] = send(kept[-1], left_to_left(2 * half - 2), mate_to_owner(half - 1))
    else:
        kept[0] = send(kept[0], left_to_left(0), mate_to_owner(0))
    for t in reversed(range(half - 1)):
        sent[t] = send(sent[t], mate_to_left(2 * t + 1), left_to_owner(t))
        if t or round_number != 1:
            u = t if round_number == 1 else t + 1
            kept[u] = send(kept[u], left_to_left(2 * u), mate_to_owner(u))
    return place_blocks(role, half, sent, kept)


def on_device(dosages, allele_counts, partner):
    cohorts, blocks = lax.axis_size("cohort"), lax.axis_size("person")
    rounds = [
        functools.partial(one_round, round_number, cohorts, blocks)
        for round_number in range(1, cohorts)
    ]
    own, counts, partner = load(dosages[0], allele_counts[0], partner)
    return lax.switch(partner[0] - 1, rounds, own, counts)


def solution(mesh):
    placed = (P("cohort", "person", None), P("cohort", "person", None), P())
    return jax.shard_map(
        on_device,
        mesh=mesh,
        in_specs=placed,
        out_specs=P("cohort", "person", None),
        check_vma=False,
    )
```

```python
import functools
import math

import jax
import jax.numpy as jnp
from jax import lax
from jax.experimental import pallas as pl
from jax.experimental.pallas import tpu as pltpu
from jax.sharding import PartitionSpec as P

AXES = ("cohort", "person")
VMEM_BYTES = 48 * 1024 * 1024
VMEM_WHOLE = 64 * 1024 * 1024
VMEM_ROOM = 128 * 1024


def left_cohorts(cohorts, round_number):
    if round_number == 1:
        return [c for c in range(cohorts) if c & 1 == 0]
    top = 1 << (round_number.bit_length() - 1)
    return [
        c
        for c in range(cohorts)
        if (c & top == 0 and c & 1 == 0) or (c & top and (c ^ round_number ^ 1) & 1 == 0)
    ]


def half_size(blocks):
    return 1 << (blocks.bit_length() // 2 - 1)


def load_kernel(count, *refs):
    sources, targets, sems = refs[:count], refs[count:-1], refs[-1]
    copies = [
        pltpu.make_async_copy(source, target, sems.at[n])
        for n, (source, target) in enumerate(zip(sources, targets))
    ]
    for copy in copies:
        copy.start()
    for copy in copies:
        copy.wait()


def load(*arrays):
    held = sum(array.size * array.dtype.itemsize for array in arrays)
    return pl.pallas_call(
        functools.partial(load_kernel, len(arrays)),
        out_shape=[pltpu.VMEM(array.shape, array.dtype) for array in arrays],
        in_specs=[pl.BlockSpec(memory_space=pl.ANY)] * len(arrays),
        out_specs=[pl.BlockSpec(memory_space=pltpu.VMEM)] * len(arrays),
        scratch_shapes=[pltpu.SemaphoreType.DMA((len(arrays),))],
        compiler_params=pltpu.CompilerParams(vmem_limit_bytes=VMEM_WHOLE - VMEM_ROOM - held),
    )(*arrays)


def sum_kernel(parts_ref, out_ref):
    total = parts_ref[0]
    for n in range(1, parts_ref.shape[0]):
        total = total + parts_ref[n]
    out_ref[...] = total


def sum_of(parts):
    vmem = pl.BlockSpec(memory_space=pltpu.VMEM)
    return pl.pallas_call(
        sum_kernel,
        out_shape=jax.ShapeDtypeStruct(parts.shape[1:], parts.dtype),
        in_specs=[vmem],
        out_specs=vmem,
        compiler_params=pltpu.CompilerParams(vmem_limit_bytes=VMEM_BYTES),
    )(parts)


def standard_rows(rows, totals, people_all):
    freq = (totals.astype(jnp.float32) + 1.0) / (2.0 * people_all + 2.0)
    scale = 1.0 / jnp.sqrt(2.0 * freq * (1.0 - freq))
    return ((rows.astype(jnp.float32) - 2.0 * freq) * scale).astype(jnp.bfloat16)


def early_kernel(count, people_all, *refs):
    (direct_ref, crossed_ref), rows, outs = refs[:2], refs[2 : count + 2], refs[count + 2 :]
    for n in range(count):
        totals_ref = crossed_ref if n == count - 1 else direct_ref
        outs[n][...] = standard_rows(rows[n][...], totals_ref[...], people_all)


def standardize(people_all, direct, crossed, wide, single):
    rows = [*wide, single]
    vmem = pl.BlockSpec(memory_space=pltpu.VMEM)
    return pl.pallas_call(
        functools.partial(early_kernel, len(rows), people_all),
        out_shape=[jax.ShapeDtypeStruct(single.shape, single.dtype)] * len(rows),
        in_specs=[vmem] * (2 + len(rows)),
        out_specs=[vmem] * len(rows),
        compiler_params=pltpu.CompilerParams(vmem_limit_bytes=VMEM_BYTES),
    )(direct, crossed, *rows)


def late_kernel(half, people_all, role_ref, *refs):
    direct_ref, crossed_ref, passed_ref = refs[:3]
    standard, relayed = refs[3 : half + 4], refs[half + 4 : 2 * half + 3]
    outs, (wide_ref, all_ref) = refs[2 * half + 3 : -2], refs[-2:]
    sent_refs, kept_refs = outs[:half], outs[half:]
    rows = passed_ref.shape[0]

    @pl.when(role_ref[0] == 1)
    def _():
        wide_ref[:rows, :] = standard[0][...]

    @pl.when(role_ref[0] == 0)
    def _():
        wide_ref[:rows, :] = standard_rows(passed_ref[...], direct_ref[...], people_all)

    all_ref[:rows, :] = standard[half][...]
    for t in range(1, half):
        at = slice(t * rows, (t + 1) * rows)
        wide_ref[at, :] = standard[t][...]
        all_ref[at, :] = standard_rows(relayed[t - 1][...], crossed_ref[...], people_all)
    dims = (((1,), (1,)), ((), ()))
    product = lax.dot_general(
        all_ref[...], wide_ref[...], dims, preferred_element_type=jnp.float32
    ) / math.sqrt(passed_ref.shape[1])
    for blocks, parts in ((product, sent_refs), (product.T, kept_refs)):
        for t in range(half):
            parts[t][...] = blocks[t * rows : (t + 1) * rows].astype(jnp.bfloat16)


def multiply(role, people_all, direct, crossed, passed, standard, relayed):
    half = len(standard) - 1
    rows, markers = passed.shape
    vmem = pl.BlockSpec(memory_space=pltpu.VMEM)
    outs = pl.pallas_call(
        functools.partial(late_kernel, half, people_all),
        out_shape=[jax.ShapeDtypeStruct((rows, half * rows), jnp.bfloat16)] * (2 * half),
        in_specs=[pl.BlockSpec(memory_space=pltpu.SMEM)] + [vmem] * (3 + 2 * half),
        out_specs=[vmem] * (2 * half),
        scratch_shapes=[pltpu.VMEM((half * rows, markers), jnp.bfloat16)] * 2,
        compiler_params=pltpu.CompilerParams(vmem_limit_bytes=VMEM_BYTES),
    )(role, direct, crossed, passed, *standard, *relayed)
    return list(outs[:half]), list(outs[half:])


def place_kernel(half, role_ref, *refs):
    sent, kept, (out_ref, whole, sems) = refs[:half], refs[half : 2 * half], refs[2 * half :]
    rows = out_ref.shape[1]
    place = role_ref[1]
    near = 2 * half
    copies = []
    for n in range(2):
        at = slice(n * rows // 2, (n + 1) * rows // 2)

        def put(block, part, column):
            to = pl.ds(pl.multiple_of(block * rows, rows), rows)
            whole[at, to] = part[at, column * rows : (column + 1) * rows]

        @pl.when(role_ref[0] == 1)
        def _():
            for t in range(half):
                for part, chip in ((kept[t], place ^ 2 * t), (sent[t], place ^ 2 * t + 1)):
                    for m in range(half):
                        put(chip ^ near * m, part, m)

        @pl.when(role_ref[0] == 0)
        def _():
            for t in range(half):
                chip = place ^ near * t
                for d in range(half):
                    put(chip ^ 2 * d, sent[t], d)
                    put(chip ^ 2 * d + 1, kept[t], d)

        copy = pltpu.make_async_copy(whole.at[at], out_ref.at[0, at], sems.at[n])
        copy.start()
        copies.append(copy)
    for copy in copies:
        copy.wait()


def place_blocks(role, half, sent, kept):
    rows = sent[0].shape[0]
    people_all = 2 * half * half * rows
    vmem = pl.BlockSpec(memory_space=pltpu.VMEM)
    return pl.pallas_call(
        functools.partial(place_kernel, half),
        out_shape=pltpu.HBM((1, rows, people_all), jnp.bfloat16),
        in_specs=[pl.BlockSpec(memory_space=pltpu.SMEM)] + [vmem] * (2 * half),
        out_specs=pl.BlockSpec(memory_space=pltpu.HBM),
        scratch_shapes=[
            pltpu.VMEM((rows, people_all), jnp.bfloat16),
            pltpu.SemaphoreType.DMA((2,)),
        ],
        compiler_params=pltpu.CompilerParams(vmem_limit_bytes=VMEM_BYTES),
    )(role, *sent, *kept)


def one_round(round_number, cohorts, blocks, own, counts):
    half = half_size(blocks)
    near = 2 * half
    left = left_cohorts(cohorts, round_number)

    def send(value, *legs):
        pairs = []
        for c in left:
            for i in range(blocks):
                for leg in legs:
                    (c0, i0), (c1, i1) = leg(c, i)
                    pairs.append((c0 * blocks + i0, c1 * blocks + i1))
        return lax.ppermute(value, AXES, pairs)

    def left_to_left(d):
        return lambda c, i: ((c, i), (c, i ^ d))

    def left_to_mate(d):
        return lambda c, i: ((c, i), (c ^ 1, i ^ d))

    def mate_to_left(d):
        return lambda c, i: ((c ^ 1, i), (c, i ^ d))

    def mate_to_mate(d):
        return lambda c, i: ((c ^ 1, i), (c ^ 1, i ^ d))

    def owner_to_left(c, i):
        return (c ^ round_number, i), (c, i)

    def owner_to_mate(c, i):
        return (c ^ round_number, i), (c ^ 1, i)

    def right_rows_to_mate(t):
        return lambda c, i: ((c ^ 1, i), (c ^ round_number, i ^ near * t))

    def right_rows_to_left(c, i):
        return (c, i), (c ^ 1 ^ round_number, i)

    def left_to_owner(t):
        return lambda c, i: ((c, i), (c ^ round_number, i ^ near * t))

    def mate_to_owner(t):
        return lambda c, i: ((c ^ 1, i), (c ^ round_number, i ^ near * t))

    cohort = lax.axis_index("cohort")
    is_left = functools.reduce(jnp.logical_or, [cohort == c for c in left])
    role = jnp.stack([is_left.astype(jnp.int32), lax.axis_index("person")])

    first = [own] + [
        send(own, left_to_left(2 * t), right_rows_to_mate(t)) for t in range(1, half)
    ]
    beside = send(own, left_to_mate(0), mate_to_left(0))
    second = [send(beside, right_rows_to_left, mate_to_mate(1))]
    counts, _ = lax.optimization_barrier((counts, beside))
    spread = jnp.broadcast_to(counts[None], (blocks, *counts.shape))
    totals = sum_of(lax.all_to_all(spread, "person", 0, 0, tiled=True))
    *first[1:], totals = lax.optimization_barrier((*first[1:], totals))
    second += [send(first[t], left_to_mate(1), mate_to_left(0)) for t in range(1, half)]
    passed = send(second[0], left_to_mate(0), mate_to_left(0))
    crossed = send(totals, left_to_mate(0), owner_to_left)
    direct = totals
    if round_number != 1:
        direct = send(totals, left_to_left(0), owner_to_mate)
    people_all = own.shape[0] * blocks
    standard = standardize(people_all, direct, crossed, first, second[0])
    sent, kept = multiply(role, people_all, direct, crossed, passed, standard, second[1:])
    sent[-1] = send(sent[-1], mate_to_left(2 * half - 1), left_to_owner(half - 1))
    if round_number == 1:
        kept[-1] = send(kept[-1], left_to_left(2 * half - 2), mate_to_owner(half - 1))
    else:
        kept[0] = send(kept[0], left_to_left(0), mate_to_owner(0))
    for t in reversed(range(half - 1)):
        sent[t] = send(sent[t], mate_to_left(2 * t + 1), left_to_owner(t))
        if t or round_number != 1:
            u = t if round_number == 1 else t + 1
            kept[u] = send(kept[u], left_to_left(2 * u), mate_to_owner(u))
    return place_blocks(role, half, sent, kept)


def on_device(dosages, allele_counts, partner):
    cohorts, blocks = lax.axis_size("cohort"), lax.axis_size("person")
    rounds = [
        functools.partial(one_round, round_number, cohorts, blocks)
        for round_number in range(1, cohorts)
    ]
    own, counts, partner = load(dosages[0], allele_counts[0], partner)
    return lax.switch(partner[0] - 1, rounds, own, counts)


def solution(mesh):
    placed = (P("cohort", "person", None), P("cohort", "person", None), P())
    return jax.shard_map(
        on_device,
        mesh=mesh,
        in_specs=placed,
        out_specs=P("cohort", "person", None),
        check_vma=False,
    )
```
